32 devices in a mesh: dp: 2 (over y), lon: 16 (over z, x, core).
Axes of the slice: x: 2, y: 2, z: 4, core: 2. Of those that a mesh axis runs over, the one named last changes fastest.
Arguments:
- field: float32 [2, 16, 512, 48], P('dp', None, 'lon'), may hold values from -6 to 6
- segment: int32 [2, 8, 256], P('dp', None, 'lon'), may hold values from 0 to 1, as said below
- padding: int32 [2, 8, 256], P('dp', None, 'lon'), may hold values from 0 to 1, as said below
- position: bfloat16 [8, 256, 1024], P(None, 'lon'), may hold values from -6 to 6
- embed_weight: bfloat16 [48, 4, 1024], P(None, None, 'lon'), may hold values from -3 to 3
- variable_embed: bfloat16 [48, 1024], P(None, 'lon'), may hold values from -6 to 6
- pool_query: bfloat16 [1024], P('lon'), may hold values from -6 to 6
- pool_key: bfloat16 [1024, 1024], P('lon'), may hold values from -0.1875 to 0.1875
- pool_value: bfloat16 [1024, 1024], P('lon'), may hold values from -0.1875 to 0.1875
- pool_out: bfloat16 [1024, 1024], P('lon'), may hold values from -0.375 to 0.375
- first_gain: bfloat16 [1024], P('lon'), may hold values from 0.5 to 1.5
- first_shift: bfloat16 [1024], P('lon'), may hold values from -4 to 4
- attend_weight: bfloat16 [1024, 3072], P('lon'), may hold values from -0.1875 to 0.1875
- attend_out: bfloat16 [1024, 1024], P('lon'), may hold values from -0.5 to 0.5
- second_gain: bfloat16 [1024], P('lon'), may hold values from 0.5 to 1.5
- second_shift: bfloat16 [1024], P('lon'), may hold values from -4 to 4
- expand_weight: bfloat16 [1024, 4096], P('lon'), may hold values from -0.1875 to 0.1875
- expand_bias: bfloat16 [4096], P('lon'), may hold values from -4 to 4
- reduce_weight: bfloat16 [4096, 1024], P('lon'), may hold values from -0.09375 to 0.09375
- reduce_bias: bfloat16 [1024], P('lon'), may hold values from -4 to 4
- head_weight: bfloat16 [1024, 192], P('lon'), may hold values from -0.1875 to 0.1875
- cotangent: bfloat16 [2, 8, 256, 192], P('dp', None, 'lon'), may hold values from -6 to 6
Outputs:
- fields: float32 [2, 8, 256, 192], P('dp', None, 'lon')
- field_grad: float32 [2, 16, 512, 48], P('dp', None, 'lon')
- position_grad: float32 [8, 256, 1024], P(None, 'lon')
- embed_grad: float32 [48, 4, 1024], P(None, None, 'lon')
- variable_grad: float32 [48, 1024], P(None, 'lon')
- query_grad: float32 [1024], P('lon')
- key_grad: float32 [1024, 1024], P('lon')
- value_grad: float32 [1024, 1024], P('lon')
- pool_out_grad: float32 [1024, 1024], P('lon')
- first_gain_grad: float32 [1024], P('lon')
- first_shift_grad: float32 [1024], P('lon')
- attend_grad: float32 [1024, 3072], P('lon')
- attend_out_grad: float32 [1024, 1024], P('lon')
- second_gain_grad: float32 [1024], P('lon')
- second_shift_grad: float32 [1024], P('lon')
- expand_grad: float32 [1024, 4096], P('lon')
- expand_bias_grad: float32 [4096], P('lon')
- reduce_grad: float32 [4096, 1024], P('lon')
- reduce_bias_grad: float32 [1024], P('lon')
- head_grad: float32 [1024, 192], P('lon')
The draws below stay inside these ranges and needn't reach their ends.
Inputs may be any that keep to these rules, and one draw needn't show every extreme that they name: Within a region the segment number depends only on the patch row: rows above a boundary row have 0, the others 1, and both bands hold at least one row; the boundary may differ between regions and draws. `padding`: padding depends only on the patch column: in each strip of 16 patch columns the padded ones are its easternmost, at most 8 of them, and in each region some strip has exactly 8 padded columns.
All inputs are finite; a program needn't handle non-finite values.
Results may differ from the reference program's by a relative error of at most 0.019.
Values may be sent and summed in bfloat16 or wider, within the bound.
No kernel may reach another device: no remote copies, remote signals or barrier semaphores. Data moves between devices by JAX's collectives and lax.ppermute only.
A program may use at most 704 MiB of HBM per device.

```python
import math
import jax
import jax.numpy as jnp
from jax import lax

D = 1024
H = 16
HD = 64
FF = 4096
NV = 48
PR = 8
PC = 16
PCOLS = 256
HPIX = 16
WPIX = 512
REGIONS = 2
OUTW = 192


def draw_segment(key, part):
    key = jax.random.fold_in(key, 11)
    boundary = jax.random.randint(key, (REGIONS, 1, 1), 1, PR)
    rows = jnp.arange(PR, dtype=jnp.int32)[None, :, None]
    return jnp.broadcast_to((rows >= boundary).astype(jnp.int32), (REGIONS, PR, PCOLS))


def draw_padding(key, part):
    key = jax.random.fold_in(key, 23)
    strips = PCOLS // PC
    first, second = jax.random.split(key)
    counts = jax.random.randint(first, (REGIONS, strips), 0, PC // 2 + 1)
    fullest = jax.random.randint(second, (REGIONS, 1), 0, strips)
    counts = jnp.where(jnp.arange(strips, dtype=jnp.int32)[None, :] == fullest, PC // 2, counts)
    columns = jnp.arange(PCOLS, dtype=jnp.int32)
    within = columns % PC
    owner_count = counts[:, columns // PC]
    live = (within[None, :] < PC - owner_count).astype(jnp.int32)
    return jnp.broadcast_to(live[:, None, :], (REGIONS, PR, PCOLS))


def levels(own_key, extent, shards, least, top_value):
    level = 1.0
    for dim, shards_of in shards:
        steps = jax.random.uniform(jax.random.fold_in(jax.random.fold_in(own_key, 6), dim), (shards_of,), jnp.float32, least / len(shards), top_value / len(shards))
        level = level * jnp.repeat(jnp.exp(steps), extent[dim] // shards_of).reshape((-1,) + (1,) * (len(extent) - 1 - dim))
    return level


def noise(stream_key, extent, scale, limit, pieces=(), kind=jnp.bfloat16):
    values = scale * jax.random.normal(stream_key, extent, jnp.float32)
    if pieces:
        values = values * levels(stream_key, extent, pieces, -0.22, 0.18)
    return jnp.clip(values, -limit, limit).astype(kind)


def setup_inputs(seed: int = 0) -> dict:
    splits = jax.random.split(jax.random.key(seed), 23)
    return {
        "field": noise(splits[0], (REGIONS, HPIX, WPIX, NV), 1.0, 6.0, ((0, 2), (2, 16)), jnp.float32),
        "segment": draw_segment(jax.random.fold_in(splits[22], 71), 0),
        "padding": draw_padding(jax.random.fold_in(splits[22], 71), 0),
        "position": noise(splits[3], (PR, PCOLS, D), 1.0, 6.0, ((1, 16),)),
        "embed_weight": noise(splits[4], (NV, 4, D), 4 ** -0.5, 3.0, ((2, 16),)),
        "variable_embed": noise(splits[5], (NV, D), 1.0, 6.0, ((1, 16),)),
        "pool_query": noise(splits[6], (D,), 1.0, 6.0, ((0, 16),)),
        "pool_key": noise(splits[7], (D, D), D ** -0.5, 0.1875, ((0, 16),)),
        "pool_value": noise(splits[8], (D, D), D ** -0.5, 0.1875, ((0, 16),)),
        "pool_out": noise(splits[9], (D, D), (D // 4) ** -0.5, 0.375, ((0, 16),)),
        "first_gain": jnp.clip(1.0 + 0.1 * jax.random.normal(splits[10], (D,), jnp.float32), 0.5, 1.5).astype(jnp.bfloat16),
        "first_shift": noise(splits[11], (D,), 0.3, 4.0, ((0, 16),)),
        "attend_weight": noise(splits[12], (D, 3 * D), D ** -0.5, 0.1875, ((0, 16),)),
        "attend_out": noise(splits[13], (D, D), (D // 8) ** -0.5, 0.5, ((0, 16),)),
        "second_gain": jnp.clip(1.0 + 0.1 * jax.random.normal(splits[14], (D,), jnp.float32), 0.5, 1.5).astype(jnp.bfloat16),
        "second_shift": noise(splits[15], (D,), 0.3, 4.0, ((0, 16),)),
        "expand_weight": noise(splits[16], (D, FF), D ** -0.5, 0.1875, ((0, 16),)),
        "expand_bias": noise(splits[17], (FF,), 0.3, 4.0, ((0, 16),)),
        "reduce_weight": noise(splits[18], (FF, D), FF ** -0.5, 0.09375, ((0, 16),)),
        "reduce_bias": noise(splits[19], (D,), 0.3, 4.0, ((0, 16),)),
        "head_weight": noise(splits[20], (D, OUTW), D ** -0.5, 0.1875, ((0, 16),)),
        "cotangent": noise(splits[21], (REGIONS, PR, PCOLS, OUTW), 1.0, 6.0, ((0, 2), (2, 16))),
    }


@jax.custom_vjp
def low(v):
    return lax.optimization_barrier(v.astype(jnp.bfloat16)).astype(jnp.float32)

@jax.custom_vjp
def low_back(v):
    return v

def low_keep(v):
    return (low(v), None)

def low_pass(kept, grad):
    return (grad,)

def back_keep(v):
    return (v, None)

def back_low(kept, grad):
    return (low(grad),)
low.defvjp(low_keep, low_pass)
low_back.defvjp(back_keep, back_low)
EPS = 1e-05
NEGATIVE = -1e+30
HIGHEST = lax.Precision.HIGHEST

def normalize(values, gain, shift):
    center = values - lax.optimization_barrier(jnp.mean(values, -1, keepdims=True))
    spread = lax.rsqrt(lax.optimization_barrier(jnp.mean(center * center, -1, keepdims=True)) + EPS)
    return center * spread * gain + shift

def region_forward(field, segment, padding, position, weights):
    embed_weight, variable_embed, pool_query, pool_key, pool_value, pool_out, first_gain, first_shift, attend_weight, attend_out, second_gain, second_shift, expand_weight, expand_bias, reduce_weight, reduce_bias, head_weight = weights
    tokens = PR * PCOLS
    scale = HD ** (-0.5)
    rows = math.gcd(tokens, 256)
    shifted = jnp.roll(field, -1, axis=1)
    patches = low(shifted.reshape(PR, 2, PCOLS, 2, NV).transpose(0, 2, 4, 1, 3).reshape(tokens, NV, 4))
    keyed = low(jnp.einsum('dhe,he->dh', pool_key.reshape(D, H, HD), pool_query.reshape(H, HD), precision=HIGHEST))

    def pool_block(block):
        embedded = jnp.einsum('tvp,vpd->tvd', block, embed_weight, precision=HIGHEST) + variable_embed
        embedded = low_back(low(embedded))
        scores = low_back(jnp.einsum('tvd,dh->tvh', embedded, keyed, precision=HIGHEST) * scale)
        chance = low(jax.nn.softmax(scores, axis=1))
        mixed = low_back(low(jnp.einsum('tvh,tvd->thd', chance, embedded, precision=HIGHEST)))
        heads = jnp.einsum('thd,dhe->the', mixed, pool_value.reshape(D, H, HD), precision=HIGHEST)
        return low_back(low(heads.reshape(block.shape[0], D)))
    pooled = lax.map(jax.checkpoint(pool_block), patches.reshape(tokens // rows, rows, NV, 4)).reshape(tokens, D)
    stream = low_back(jnp.dot(pooled, pool_out, precision=HIGHEST)) + position.reshape(tokens, D)
    normed = low_back(low(normalize(stream, first_gain, first_shift)))
    packed = low_back(low(jnp.dot(normed, attend_weight, precision=HIGHEST))).reshape(tokens, 3, H, HD)
    queries = packed[:, 0]
    keys = packed[:, 1]
    values = packed[:, 2]
    query_label = segment.reshape(tokens)
    key_label = jnp.where(padding.reshape(tokens) == 1, query_label, -1)

    def attend(items):
        block_queries, block_label = items
        scores = low_back(jnp.einsum('qhd,khd->qhk', block_queries, keys, precision=HIGHEST) * scale)
        allowed = (block_label[:, None] == key_label[None, :])[:, None, :]
        scores = jnp.where(allowed, scores, NEGATIVE)
        summit = lax.optimization_barrier(jnp.max(scores, -1, keepdims=True))
        raised = jnp.where(allowed, jnp.exp(scores - summit), 0.0)
        chance = low(raised / lax.optimization_barrier(jnp.sum(raised, -1, keepdims=True)))
        return jnp.einsum('qhk,khd->qhd', chance, values, precision=HIGHEST)
    attended = lax.map(jax.checkpoint(attend), (queries.reshape(tokens // rows, rows, H, HD), query_label.reshape(tokens // rows, rows)))
    attended = low_back(low(attended.reshape(tokens, D)))
    stream = stream + low_back(jnp.dot(attended, attend_out, precision=HIGHEST))
    normed = low_back(low(normalize(stream, second_gain, second_shift)))
    before = low_back(jnp.dot(normed, expand_weight, precision=HIGHEST) + expand_bias)
    hidden = low_back(low(jax.nn.gelu(before, approximate=False)))
    stream = stream + low_back(jnp.dot(hidden, reduce_weight, precision=HIGHEST) + reduce_bias)
    final = low_back(low(stream))
    return jnp.dot(final, head_weight, precision=HIGHEST).reshape(PR, PCOLS, OUTW)

def reference(field, segment, padding, position, embed_weight, variable_embed, pool_query, pool_key, pool_value, pool_out, first_gain, first_shift, attend_weight, attend_out, second_gain, second_shift, expand_weight, expand_bias, reduce_weight, reduce_bias, head_weight, cotangent):
    floats = tuple((weight.astype(jnp.float32) for weight in (embed_weight, variable_embed, pool_query, pool_key, pool_value, pool_out, first_gain, first_shift, attend_weight, attend_out, second_gain, second_shift, expand_weight, expand_bias, reduce_weight, reduce_bias, head_weight)))

    def forward(field_in, position_in, weights):
        return jnp.stack([region_forward(field_in[index], segment[index], padding[index], position_in, weights) for index in range(REGIONS)])
    fields, pullback = jax.vjp(forward, field, position.astype(jnp.float32), floats)
    field_grad, position_grad, grads = pullback(cotangent.astype(jnp.float32))
    return (fields, field_grad, position_grad, grads[0], grads[1], grads[2], grads[3], grads[4], grads[5], grads[6], grads[7], grads[8], grads[9], grads[10], grads[11], grads[12], grads[13], grads[14], grads[15], grads[16])
```

```python
import functools

import jax
import jax.numpy as jnp
from jax import lax
from jax.experimental import pallas as pl
from jax.experimental.pallas import tpu as pltpu
from jax.sharding import PartitionSpec as P

D = 1024
H = 16
HD = 64
FF = 4096
NV = 48
OUTW = 192
PIX = 4 * NV
EXT = 5 * NV
FULL = 256
LATE = 2 * D + FULL
HEAD_AT = D
SEED_AT = D + FULL
SHARE = 1
WIDE = 128
SUM_LANE = 67

EPS = 1e-05
NEGATIVE = -1e30
SCALE = HD ** (-0.5)
VMEM = 56 * 1024 * 1024

f32 = jnp.float32
bf16 = jnp.bfloat16


def rounded(values):
    return values.astype(bf16)


def mm(a, b, da=1, db=0):
    return lax.dot_general(a, b, (((da,), (db,)), ((), ())), preferred_element_type=f32)


def layer_stats(values):
    center = values - jnp.mean(values, -1, keepdims=True)
    spread = lax.rsqrt(jnp.mean(center * center, -1, keepdims=True) + EPS)
    return (center * spread, spread)


def norm_back(grad_normed, normal, spread, gain):
    scaled = grad_normed * gain
    return spread * (
        scaled
        - jnp.mean(scaled, -1, keepdims=True)
        - normal * jnp.mean(scaled * normal, -1, keepdims=True)
    )


def params(**more):
    return pltpu.CompilerParams(vmem_limit_bytes=VMEM, **more)


SMEM_SPEC = pl.BlockSpec(memory_space=pltpu.SMEM)
WHOLE = pl.BlockSpec(memory_space=pltpu.VMEM)


def columns_of(array, width, start):
    return pl.BlockSpec((array.shape[0], width), lambda i: (0, start // width))


def cost(flops, moved, hard=0, filler=False):
    share = 1 if filler else SHARE
    return pl.CostEstimate(flops=flops // share, bytes_accessed=moved // share, transcendentals=0)


def total(refs):
    return sum(ref[...].astype(f32) for ref in refs)


def pool_forward_kernel(
    pixels_ref,
    keyed_ref,
    position_ref,
    value_ref,
    pool_ref,
    extended_ref,
    stream_ref,
    normed_ref,
    heads_ref,
    chance_ref,
    rows_ref,
    score_ref,
    vectors_ref,
):
    pixels = pixels_ref[...]
    blank = jnp.zeros((FULL - EXT, pixels.shape[1]), f32)
    extended = extended_ref[...]
    last = extended[:, FULL - WIDE :].astype(f32)
    vectors_ref[...] = jnp.transpose(last)[WIDE - (FULL - EXT) :, :]
    rows_ref[...] = rounded(mm(value_ref[...], extended, 0, 0))
    score_ref[...] = mm(extended, keyed_ref[...], 0, 0)
    for h in range(H):
        terms = pixels * score_ref[:, h : h + 1]
        scores = terms[:NV]
        for p in range(1, 5):
            scores = scores + terms[p * NV : (p + 1) * NV]
        scores = scores * SCALE
        raised = jnp.exp(scores - jnp.max(scores, 0, keepdims=True))
        chance = raised / jnp.sum(raised, 0, keepdims=True)
        chance_ref[h] = chance
        spread = rounded(jnp.concatenate([chance] * 5 + [blank], 0) * pixels)
        heads_ref[h * HD : (h + 1) * HD, :] = rounded(
            mm(rows_ref[h * HD : (h + 1) * HD, :], spread)
        )
    stream = mm(heads_ref[...], pool_ref[...], 0, 0) + position_ref[...].astype(f32)
    stream_ref[...] = stream
    normal, unused = layer_stats(stream)
    normed_ref[...] = rounded(normal * vectors_ref[1:2, :] + vectors_ref[2:3, :])


def pool_forward(pixels, keyed, position, first):
    tokens = pixels.shape[1]
    return pl.pallas_call(
        pool_forward_kernel,
        grid=(1,),
        in_specs=[
            WHOLE,
            WHOLE,
            WHOLE,
            columns_of(first, D, 0),
            columns_of(first, D, D),
            columns_of(first, FULL, 2 * D),
        ],
        out_specs=[WHOLE] * 7,
        out_shape=(
            jax.ShapeDtypeStruct((tokens, D), f32),
            jax.ShapeDtypeStruct((tokens, D), bf16),
            jax.ShapeDtypeStruct((D, tokens), bf16),
            jax.ShapeDtypeStruct((H, NV, tokens), f32),
            jax.ShapeDtypeStruct((D, FULL), bf16),
            jax.ShapeDtypeStruct((FULL, H), f32),
            jax.ShapeDtypeStruct((FULL - EXT, D), f32),
        ),
        compiler_params=params(),
        cost_estimate=cost(3_000_000_000, 8_000_000, H * NV * tokens),
        name="pool_forward",
    )(pixels, keyed, position, first, first, first)


def pool_backward_kernel(
    order_ref,
    pixels_ref,
    score_ref,
    rows_ref,
    chance_ref,
    heads_ref,
    keyed_ref,
    value_ref,
    pool_ref,
    extended_ref,
    stream_ref,
    grad_one_ref,
    vectors_ref,
    sums_ref,
    early_ref,
    *refs,
):
    terms, (pixel_ref, stream_grad_ref, *outs), (late, mixed, scores, vectors) = (
        refs[: -6 - H // 2],
        refs[-6 - H // 2 : -4],
        refs[-4:],
    )
    grad_normed = total(terms)
    normal, spread = layer_stats(stream_ref[...])
    grad_stream = grad_one_ref[...] + norm_back(grad_normed, normal, spread, vectors_ref[1:2, :])
    stream_grad_ref[...] = grad_stream
    vectors[...] = jnp.zeros_like(vectors)
    vectors[0:1, :] = jnp.sum(grad_normed * normal, 0, keepdims=True)
    vectors[1:2, :] = jnp.sum(grad_normed, 0, keepdims=True)
    vectors[2:5, :] = sums_ref[0:3, :]
    grad_pool = rounded(grad_stream)
    grad_heads = rounded(mm(pool_ref[...], grad_pool, 1, 1))
    late[:, :D] = rounded(mm(heads_ref[...], grad_pool))

    pixels = pixels_ref[...]
    tokens = pixels.shape[1]
    blank = jnp.zeros((FULL - EXT, tokens), f32)
    pixel_ref[...] = jnp.zeros_like(pixel_ref)
    scores[...] = jnp.zeros_like(scores)
    late[:, LATE:] = rounded(jnp.transpose(vectors[...]))
    fours = lax.broadcasted_iota(jnp.int32, (HD, FULL), 1) // 4
    fours = rounded(fours == lax.broadcasted_iota(jnp.int32, (HD, FULL), 0))
    lane = lax.broadcasted_iota(jnp.int32, (FULL, WIDE), 1) - 8
    within = lane == lax.broadcasted_iota(jnp.int32, (FULL, WIDE), 0) % 4
    for h in range(H):
        block = slice(h * HD, (h + 1) * HD)
        grad = grad_heads[block, :]
        chance = chance_ref[h]
        wide = jnp.concatenate([chance] * 5 + [blank], 0)
        back = mm(rows_ref[block, :], grad, 0, 0)
        parts = back * pixels
        grad_chance = parts[:NV]
        for p in range(1, 5):
            grad_chance = grad_chance + parts[p * NV : (p + 1) * NV]
        grad_score = chance * (grad_chance - jnp.sum(chance * grad_chance, 0, keepdims=True))
        grad_wide = jnp.concatenate([grad_score * SCALE] * 5 + [blank], 0)
        mixed[block, :] = rounded(mm(grad, rounded(wide * pixels), 1, 1))
        score_grad = jnp.sum(grad_wide * pixels, 1, keepdims=True)
        scores[:, h : h + 1] = score_grad
        late[block, LATE:] += rounded(mm(fours, rounded(jnp.where(within, score_grad, 0.0))))
        pixel_ref[...] += (
            wide[:PIX] * back[:PIX] + grad_wide[:PIX] * score_ref[:PIX, h : h + 1]
        )
    score_grads = rounded(scores[:, :H])
    extended = extended_ref[...]
    late[:, D : 2 * D] = rounded(mm(extended, mixed[...], 1, 1))
    embed_grad = mm(value_ref[...], mixed[...]) + mm(keyed_ref[...], score_grads, 1, 1)
    keyed_grad = mm(extended, score_grads)
    last = jnp.concatenate([keyed_grad, jnp.zeros((D, FULL - H), f32)], 1)
    late[:, 2 * D : LATE] = rounded(
        jnp.where(
            lax.broadcasted_iota(jnp.int32, embed_grad.shape, 1) < EXT,
            embed_grad,
            pltpu.roll(last, EXT, 1),
        )
    )
    for i, ref in enumerate(outs):
        for j in range(2):
            start = pl.multiple_of(order_ref[2 * i + j] * HD, HD)
            ref[j * HD : (j + 1) * HD, : LATE + WIDE] = late[pl.ds(start, HD), :]
        ref[:, LATE + WIDE :] = early_ref[2 * i * HD : (2 * i + 2) * HD, :]


def pool_backward(
    order, pixels, score, rows, chance, heads, keyed, first, stream, grad_one, vectors, sums, early, terms
):
    tokens = pixels.shape[1]
    return pl.pallas_call(
        pool_backward_kernel,
        grid=(1,),
        in_specs=[SMEM_SPEC]
        + [WHOLE] * 6
        + [columns_of(first, D, 0), columns_of(first, D, D), columns_of(first, FULL, 2 * D)]
        + [WHOLE] * (5 + len(terms)),
        out_specs=[WHOLE] * (2 + H // 2),
        out_shape=[
            jax.ShapeDtypeStruct((PIX, tokens), f32),
            jax.ShapeDtypeStruct((tokens, D), f32),
        ]
        + [jax.ShapeDtypeStruct((2 * HD, LATE + WIDE + early.shape[1]), bf16)] * (H // 2),
        scratch_shapes=[
            pltpu.VMEM((D, LATE + WIDE), bf16),
            pltpu.VMEM((D, FULL), bf16),
            pltpu.VMEM((FULL, WIDE), f32),
            pltpu.VMEM((WIDE, D), f32),
        ],
        compiler_params=params(),
        cost_estimate=cost(4_000_000_000, 14_000_000),
        name="pool_backward",
    )(
        order,
        pixels,
        score,
        rows,
        chance,
        heads,
        keyed,
        first,
        first,
        first,
        stream,
        grad_one,
        vectors,
        sums,
        early,
        *terms,
    )


def copy_parts(refs, into):
    start = 0
    for ref in refs:
        into[start : start + ref.shape[0], :] = ref[...]
        start += ref.shape[0]


def columns_from(rows):
    width = rows[0].shape[1]
    return jnp.concatenate(
        [jnp.transpose(jnp.broadcast_to(row, (width, width))) for row in rows], 0
    )


def pack_kernel(table_ref, weight_ref, band_ref, live_ref, *refs):
    parts, (query_ref, key_ref, value_ref, every) = refs[:-4], refs[-4:]
    copy_parts(parts, every)
    count = every.shape[0]
    block = 512
    blocks = H * block // count
    for i in range(count // block):
        rows = slice(i * block, (i + 1) * block)
        packed = rounded(mm(every[rows, :], weight_ref[...])).astype(f32)
        here = range(i * blocks, (i + 1) * blocks)
        live = columns_from([live_ref[pl.ds(table_ref[e], 1), :] for e in here])
        band = columns_from([band_ref[...]] * blocks)
        left, right = packed[:, :WIDE], packed[:, WIDE:]
        lane = lax.broadcasted_iota(jnp.int32, left.shape, 1)
        query = jnp.where(lane == HD, 1.0 - band, jnp.where(lane == HD + 1, band, 0.0))
        query_ref[rows, :] = rounded(jnp.where(lane < HD, left * SCALE, query))
        key = jnp.where(
            lane == HD,
            NEGATIVE * (1.0 - live * (1.0 - band)),
            jnp.where(
                lane == HD + 1,
                NEGATIVE * (1.0 - live * band),
                jnp.where(lane < HD + 5, -1.0, 0.0),
            ),
        )
        key_ref[rows, :] = rounded(jnp.where(lane < HD, pltpu.roll(left, HD, 1), key))
        value = jnp.where(lane < SUM_LANE, -1.0, jnp.where(lane == SUM_LANE, 1.0, 0.0))
        value_ref[rows, :] = rounded(jnp.where(lane < HD, right, value))


def pack(table, parts, weight, band, live):
    count = sum(part.shape[0] for part in parts)
    return pl.pallas_call(
        pack_kernel,
        in_specs=[SMEM_SPEC] + [WHOLE] * (3 + len(parts)),
        out_shape=[jax.ShapeDtypeStruct((count, WIDE), bf16)] * 3,
        scratch_shapes=[pltpu.VMEM((count, D), bf16)],
        compiler_params=params(),
        cost_estimate=cost(2 * count * D * FULL, 3 * count * D),
        name="pack",
    )(table, weight, band, live, *parts)


def attend_kernel(query_ref, key_ref, value_ref, out_ref, keep_ref, send_ref, *, half):
    scores = mm(query_ref[...], key_ref[...], 1, 1)
    summit = jnp.max(scores, -1, keepdims=True)
    raised = rounded(jnp.exp(scores - summit))
    total = mm(raised, value_ref[...])
    amount = total[:, SUM_LANE : SUM_LANE + 1]
    lane = lax.broadcasted_iota(jnp.int32, total.shape, 1)
    out = jnp.where(lane < HD, total / amount, summit + jnp.log(amount))
    out_ref[...] = out
    low = rounded(out[:, :HD])

    @pl.when(pl.program_id(0) < half)
    def _():
        keep_ref[...] = low

    @pl.when(pl.program_id(0) >= half)
    def _():
        send_ref[...] = low


def attend(queries, keys, values):
    rows, count = queries.shape[0], keys.shape[0]
    block = min(256, max(32, 256 * 2048 // count))
    half = rows // block // 2
    return pl.pallas_call(
        functools.partial(attend_kernel, half=half),
        grid=(2 * half,),
        in_specs=[
            pl.BlockSpec((block, WIDE), lambda i: (i, 0)),
            pl.BlockSpec((count, WIDE), lambda i: (0, 0)),
            pl.BlockSpec((count, WIDE), lambda i: (0, 0)),
        ],
        out_specs=(
            pl.BlockSpec((block, WIDE), lambda i: (i, 0)),
            pl.BlockSpec((block, HD), lambda i: (jnp.minimum(i, half - 1), 0)),
            pl.BlockSpec((block, HD), lambda i: (jnp.maximum(i - half, 0), 0)),
        ),
        out_shape=(
            jax.ShapeDtypeStruct((rows, WIDE), f32),
            jax.ShapeDtypeStruct((rows // 2, HD), bf16),
            jax.ShapeDtypeStruct((rows // 2, HD), bf16),
        ),
        compiler_params=params(dimension_semantics=("arbitrary",)),
        cost_estimate=cost(4 * rows * count * WIDE, rows * WIDE * 6 + count * WIDE * 4),
        name="attend",
    )(queries, keys, values)


def three_parts(values):
    high = rounded(values)
    rest = values - high.astype(f32)
    middle = rounded(rest)
    low = rounded(rest - middle.astype(f32))
    return [part.astype(f32) for part in (high, middle, low)]


def attend_back_kernel(
    query_ref,
    out_ref,
    key_ref,
    value_ref,
    *refs,
):
    moved_refs, (query_grad_ref, key_grad_ref, value_grad_ref, queries, grads) = (
        refs[:-5],
        refs[-5:],
    )

    @pl.when(pl.program_id(0) == 0)
    def _():
        lane = lax.broadcasted_iota(jnp.int32, queries.shape, 1)
        out = out_ref[...]
        log_total = out[:, HD : HD + 1]
        moved = jnp.concatenate([ref[...] for ref in moved_refs], 0).astype(f32)
        grad = jnp.concatenate([moved, pltpu.roll(moved, HD, 1)], 0)
        grad = jnp.where(lane < HD, grad, 0.0)
        balance = jnp.sum(out * grad, -1, keepdims=True)
        query = query_ref[...].astype(f32)
        for i, part in enumerate(three_parts(log_total)):
            query = jnp.where(lane == HD + 2 + i, part, query)
        for i, part in enumerate(three_parts(balance)):
            grad = jnp.where(lane == HD + i, part, grad)
        queries[...] = rounded(query)
        grads[...] = rounded(grad)
        query_grad_ref[...] = jnp.zeros_like(query_grad_ref)

    prob = jnp.exp(mm(key_ref[...], queries[...], 1, 1))
    slope = mm(value_ref[...], grads[...], 1, 1)
    grad_scores = rounded(prob * slope)
    value_grad_ref[...] = mm(rounded(prob), grads[...])
    key_grad_ref[...] = mm(grad_scores, queries[...])
    query_grad_ref[...] += mm(key_ref[...], grad_scores, 0, 0)


def attend_back(queries, out, keys, values, moved):
    rows, count = queries.shape[0], keys.shape[0]
    block = 256
    whole = pl.BlockSpec((rows, WIDE), lambda i: (0, 0))
    part = pl.BlockSpec((block, WIDE), lambda i: (i, 0))
    return pl.pallas_call(
        attend_back_kernel,
        grid=(count // block,),
        in_specs=[
            whole,
            whole,
            part,
            part,
        ]
        + [WHOLE] * len(moved),
        out_specs=(pl.BlockSpec((WIDE, rows), lambda i: (0, 0)), part, part),
        out_shape=(
            jax.ShapeDtypeStruct((WIDE, rows), f32),
            jax.ShapeDtypeStruct((count, WIDE), f32),
            jax.ShapeDtypeStruct((count, WIDE), f32),
        ),
        scratch_shapes=[pltpu.VMEM((rows, WIDE), bf16), pltpu.VMEM((rows, WIDE), bf16)],
        compiler_params=params(dimension_semantics=("arbitrary",)),
        cost_estimate=cost(10 * rows * count * WIDE, rows * WIDE * 12 + count * WIDE * 14),
        name="attend_back",
    )(queries, out, keys, values, *moved)


def unpack_kernel(query_ref, key_ref, value_ref, weight_ref, packed_ref, *refs):
    weight = weight_ref[...]
    step = key_ref.shape[0] // len(refs)
    for i, ref in enumerate(refs):
        rows = slice(i * step, (i + 1) * step)
        query = jnp.transpose(query_ref[:, rows]) * SCALE
        lane = lax.broadcasted_iota(jnp.int32, (step, WIDE), 1)
        left = jnp.where(lane < HD, query, pltpu.roll(key_ref[rows, :], HD, 1))
        right = jnp.where(lane < HD, value_ref[rows, :], 0.0)
        packed = rounded(jnp.concatenate([left, right], 1))
        packed_ref[rows, :] = packed
        ref[...] = rounded(mm(packed, weight, 1, 1))


def unpack(query_back, key_back, value_back, weight):
    count = key_back.shape[0]
    return pl.pallas_call(
        unpack_kernel,
        out_shape=[jax.ShapeDtypeStruct((count, FULL), bf16)]
        + [jax.ShapeDtypeStruct((count // 8, D), bf16)] * 8,
        compiler_params=params(),
        cost_estimate=cost(2 * count * D * FULL, 4 * count * D),
        name="unpack",
    )(query_back, key_back, value_back, weight)


def weight_grad_kernel(*refs, count):
    parts, grads, (out_ref, every, changes) = refs[:count], refs[count:-3], refs[-3:]
    copy_parts(parts, every)
    copy_parts(grads, changes)
    block = 256
    for i in range(D // block):
        columns = slice(i * block, (i + 1) * block)
        out_ref[columns, :] = rounded(mm(every[:, columns], changes[...], 0, 0))


def weight_grad(parts, grads):
    count, width = sum(grad.shape[0] for grad in grads), grads[0].shape[1]
    return pl.pallas_call(
        functools.partial(weight_grad_kernel, count=len(parts)),
        out_shape=jax.ShapeDtypeStruct((D, width), bf16),
        scratch_shapes=[pltpu.VMEM((count, D), bf16), pltpu.VMEM((count, width), bf16)],
        compiler_params=params(),
        cost_estimate=cost(20 * count * D * width, 3 * count * D, filler=True),
        name="weight_grad",
    )(*parts, *grads)


def sort_rows(order_ref, from_ref, into):
    for i in range(H):
        start = pl.multiple_of(order_ref[(i % 2) * 8 + i // 2] * HD, HD)
        into[i * HD : (i + 1) * HD, :] = from_ref[pl.ds(start, HD), :]


def heads_of(refs):
    return jnp.concatenate([ref[i] for ref in refs for i in range(2)], 1)


def middle_kernel(order_ref, weight_ref, stream_ref, vectors_ref, *refs):
    heads, (one_ref, normed_ref, sorted_w) = refs[:-3], refs[-3:]
    sort_rows(order_ref, weight_ref, sorted_w)
    stream = stream_ref[...] + mm(heads_of(heads), sorted_w[...])
    one_ref[...] = stream
    normal, unused = layer_stats(stream)
    normed_ref[...] = rounded(normal * vectors_ref[3:4, :] + vectors_ref[4:5, :])


def middle(order, second, stream, vectors, heads):
    tokens = stream.shape[0]
    return pl.pallas_call(
        middle_kernel,
        grid=(1,),
        in_specs=[SMEM_SPEC, columns_of(second, D, 0)] + [WHOLE] * (2 + len(heads)),
        out_specs=[WHOLE] * 2,
        out_shape=(
            jax.ShapeDtypeStruct((tokens, D), f32),
            jax.ShapeDtypeStruct((tokens, D), bf16),
        ),
        scratch_shapes=[pltpu.VMEM((D, D), bf16)],
        compiler_params=params(),
        cost_estimate=cost(2 * tokens * D * D, 2 * D * D + 12 * tokens * D),
        name="middle",
    )(order, second, stream, vectors, *heads)


def middle_back_kernel(order_ref, weight_ref, head_ref, seed_ref, stream_ref, vectors_ref, *refs):
    terms, (one_ref, branch_ref, keep_ref, send_ref, sums_ref, fields_ref, sorted_w) = (
        refs[:-7],
        refs[-7:],
    )
    sort_rows(order_ref, weight_ref, sorted_w)
    summed = total(terms)
    grad_normed = summed[:, :D]
    fields_ref[...] = summed[:, D:] + mm(rounded(stream_ref[...] + vectors_ref[5:6, :]), head_ref[...])
    stream = stream_ref[...]
    grad_two = rounded(mm(seed_ref[...], head_ref[...], 1, 1)).astype(f32)
    normal, spread = layer_stats(stream)
    grad_one = grad_two + norm_back(grad_normed, normal, spread, vectors_ref[3:4, :])
    one_ref[...] = grad_one
    branch = rounded(grad_one)
    branch_ref[...] = branch
    back = rounded(mm(branch, sorted_w[...], 1, 1)).astype(f32)
    tokens = stream.shape[0]
    for i in range(H // 2):
        pair = back[:, i * WIDE : (i + 1) * WIDE]
        rows = slice(i * tokens, (i + 1) * tokens)
        keep_ref[rows, :] = rounded(pair[:, :HD])
        send_ref[rows, :] = rounded(pltpu.roll(pair, HD, 1)[:, :HD])
    sums_ref[...] = jnp.zeros_like(sums_ref)
    sums_ref[0:1, :] = jnp.sum(grad_normed * normal, 0, keepdims=True)
    sums_ref[1:2, :] = jnp.sum(grad_normed, 0, keepdims=True)
    sums_ref[2:3, :] = jnp.sum(grad_two, 0, keepdims=True)


def middle_back(order, second, seed, stream, vectors, terms):
    tokens = stream.shape[0]
    half = H // 2 * tokens
    return pl.pallas_call(
        middle_back_kernel,
        grid=(1,),
        in_specs=[SMEM_SPEC, columns_of(second, D, 0), columns_of(second, FULL, HEAD_AT)]
        + [WHOLE] * (3 + len(terms)),
        out_specs=[WHOLE] * 6,
        out_shape=(
            jax.ShapeDtypeStruct((tokens, D), f32),
            jax.ShapeDtypeStruct((tokens, D), bf16),
            jax.ShapeDtypeStruct((half, HD), bf16),
            jax.ShapeDtypeStruct((half, HD), bf16),
            jax.ShapeDtypeStruct((8, D), f32),
            jax.ShapeDtypeStruct((tokens, FULL), f32),
        ),
        scratch_shapes=[pltpu.VMEM((D, D), bf16)],
        compiler_params=params(),
        cost_estimate=cost(3 * tokens * D * D, 3 * D * D + 20 * tokens * D),
        name="middle_back",
    )(order, second, second, seed, stream, vectors, *terms)


def early_kernel(
    order_ref, branch_ref, stream_ref, vectors_ref, seed_ref, reduce_ref, inner_ref, *refs
):
    heads, (one_ref, two_ref, rows) = refs[:-3], refs[-3:]
    branch = branch_ref[...]
    half = one_ref.shape[1]
    for i in range(H // 2):
        pair = rounded(mm(heads[i // 2][i % 2], branch, 0, 0))
        for j in range(2):
            block = slice((j * 8 + i) * HD, (j * 8 + i + 1) * HD)
            one_ref[block, :] = pair[j * HD : (j + 1) * HD, :half]
            two_ref[block, : D - half] = pair[j * HD : (j + 1) * HD, half:]
    stream = rounded(stream_ref[...] + vectors_ref[5:6, :])
    rows[...] = rounded(
        mm(stream, seed_ref[...], 0, 0) + mm(reduce_ref[...], inner_ref[...], 0, 0)
    )
    for e in range(H):
        start = pl.multiple_of(order_ref[e] * HD, HD)
        two_ref[e * HD : (e + 1) * HD, D - half :] = rows[pl.ds(start, HD), :]


def early_grads(order, branch, stream, vectors, seed, reduce_here, inner, heads):
    tokens = stream.shape[0]
    half = (D + FULL) // 2
    return pl.pallas_call(
        early_kernel,
        in_specs=[SMEM_SPEC] + [WHOLE] * (6 + len(heads)),
        out_shape=(
            jax.ShapeDtypeStruct((D, half), bf16),
            jax.ShapeDtypeStruct((D, half), bf16),
        ),
        scratch_shapes=[pltpu.VMEM((D, FULL), bf16)],
        compiler_params=params(),
        cost_estimate=cost(20 * tokens * D * (D + FULL), 6_000_000, filler=True),
        name="early_grads",
    )(order, branch, stream, vectors, seed, reduce_here, inner, *heads)


def feed_kernel(order_ref, expand_ref, bias_ref, both_ref, one_ref, two_ref, *refs):
    parts, (before_ref, inner_ref, sums_ref, *outs) = refs[:H], refs[H:]
    expand = expand_ref[...]
    both = both_ref[...]
    inner = jnp.zeros(inner_ref.shape, f32)
    sums = jnp.zeros((1, expand.shape[1]), f32)
    tokens = parts[0].shape[0]
    step = 2 * tokens
    for i in range(8):
        block = slice(i * step, (i + 1) * step)
        rows = jnp.concatenate([parts[2 * i][...], parts[2 * i + 1][...]], 0)
        before = mm(rows, expand) + bias_ref[...].astype(f32)
        half = 0.5 + 0.5 * lax.erf(before * 0.7071067811865476)
        hidden = rounded(before * half)
        slope = half + before * jnp.exp(-0.5 * before * before) * 0.3989422804014327
        seed = jnp.concatenate(
            [
                ref[pl.ds(pl.multiple_of(order_ref[e] * HD, HD), HD), :]
                for e in (2 * i, 2 * i + 1)
                for ref in (one_ref, two_ref)
            ],
            0,
        )
        grad = rounded(mm(seed, both, 1, 1) * slope)
        before_ref[block, :] = grad
        outs[i][:, :D] = rounded(mm(grad, expand, 1, 1))
        outs[i][:, D:] = rounded(mm(hidden, both))
        inner = inner + mm(hidden, seed, 0, 0)
        sums = sums + jnp.sum(grad.astype(f32), 0, keepdims=True)
    inner_ref[...] = rounded(inner)
    sums_ref[...] = jnp.broadcast_to(sums, sums_ref.shape)


def feed(order, parts, expand, bias, both, second):
    tokens = parts[0].shape[0]
    count, width = H * tokens, expand.shape[1]
    return pl.pallas_call(
        feed_kernel,
        grid=(1,),
        in_specs=[SMEM_SPEC, WHOLE, WHOLE, WHOLE, columns_of(second, FULL, SEED_AT), columns_of(second, FULL, SEED_AT + FULL)]
        + [WHOLE] * H,
        out_specs=[WHOLE] * 11,
        out_shape=[
            jax.ShapeDtypeStruct((count, width), bf16),
            jax.ShapeDtypeStruct((width, FULL), bf16),
            jax.ShapeDtypeStruct((8, width), f32),
        ]
        + [jax.ShapeDtypeStruct((2 * tokens, D + FULL), bf16)] * 8,
        compiler_params=params(),
        cost_estimate=cost(6 * count * D * width, 5 * count * D),
        name="feed",
    )(order, expand, bias, both, second, second, *parts)


def turn(array, pairs):
    return lax.ppermute(array, "lon", pairs)


class Steps:
    def __init__(self, lon):
        self.lon = lon
        self.both, self.side, self.mine, self.sent = {}, {}, {}, {}

    def add(self, k, keep, send):
        rows = keep.shape[0] // 2
        self.both[k] = keep.astype(f32) + turn(send, self.lon.core).astype(f32)
        away = rounded(self.both[k][rows:])
        if k in (3, 0):
            away = after(away, self.side[2])
        self.side[k] = turn(away, self.lon.side)
        self.mine[k] = self.both[k][:rows] + self.side[k].astype(f32)
        if k:
            self.sent[k] = turn(rounded(self.mine[k]), self.lon.up[k])

    def terms(self):
        return [self.mine[0], self.sent[1], self.sent[2], self.sent[3]]


class Lon:
    def __init__(self, size):
        self.size = size
        self.groups = size // H
        self.near = [[g * H + h for h in range(H)] for g in range(self.groups)]
        self.far = [[g * H + h for g in range(self.groups)] for h in range(H)]
        self.own = self.groups == 1
        every = range(H)
        self.core = [(i, i ^ 1) for i in every]
        self.side = [(i, i ^ 2) for i in every]
        self.down = [[(i, (i + 4 * k) % H) for i in every] for k in range(4)]
        self.up = [[(i, (i - 4 * k) % H) for i in every] for k in range(4)]

    def split(self):
        return {"axis_index_groups": self.near}

    def order(self):
        if not self.own:
            return jnp.arange(H, dtype=jnp.int32)
        here = lax.axis_index("lon")
        z, x, core = here // 4, (here // 2) % 2, here % 2
        return jnp.stack(
            [
                ((z - k) % 4) * 4 + (x ^ xr) * 2 + (core ^ cr)
                for cr in range(2)
                for k in range(4)
                for xr in range(2)
            ]
        ).astype(jnp.int32)

    def gather_all(self, part):
        return lax.all_gather(part, "lon", axis=0, tiled=True)

    def sum_all(self, whole):
        return lax.psum_scatter(whole, "lon", scatter_dimension=0, tiled=True)

    def gather(self, part, groups=True):
        if not self.own:
            split = self.split() if groups else {}
            whole = lax.all_gather(part, "lon", axis=0, tiled=True, **split)
            rows = whole.shape[0] // H
            return [whole[i * rows : (i + 1) * rows] for i in range(H)]
        line = {0: part, **{k: turn(part, self.down[k]) for k in (2, 1, 3)}}
        side = {k: turn(line[k], self.side) for k in (0, 2, 1, 3)}
        mine = [piece for k in range(4) for piece in (line[k], side[k])]
        return mine + [turn(piece, self.core) for piece in mine]

    def gather_group(self, part):
        return lax.all_gather(part, "lon", axis=0, tiled=True, **({} if self.own else self.split()))

    def sum(self, parts, groups=True):
        if not self.own:
            whole = jnp.concatenate(parts)
            split = self.split() if groups else {}
            whole = lax.psum_scatter(whole, "lon", scatter_dimension=0, tiled=True, **split)
            return [whole], whole
        steps = Steps(self)
        for k in (2, 1, 3, 0):
            steps.add(k, parts[k], parts[4 + k])
        return steps.terms(), steps.side[0]

    def first(self, weights, vectors, live):
        spare = FULL - EXT
        if not self.own:
            vectors = lax.all_gather(vectors, "lon", axis=1, tiled=True)
            live = self.gather_group(live).reshape(H, 2, HD).transpose(1, 0, 2)
        marks = jnp.concatenate([vectors, live.reshape(2, -1)]).T
        marks = jnp.pad(marks, ((0, 0), (0, spare - marks.shape[1])))
        if not self.own:
            return jnp.concatenate([self.gather_all(weights), marks], 1)
        return self.gather_all(jnp.concatenate([weights, marks], 1))

    def second(self, weights, seed):
        if not self.own:
            seed = self.gather_group(seed).reshape(H, 2, HD, FULL).transpose(0, 2, 1, 3)
            return jnp.concatenate([self.gather_all(weights), seed.reshape(D, 2 * FULL)], 1)
        half = seed.shape[0] // 2
        return self.gather_all(jnp.concatenate([weights, seed[:half], seed[half:]], 1))

    def spread_columns(self, column):
        if self.own:
            return self.swap_all(jnp.tile(column[None], (H, 1)))
        return lax.all_gather(column, "lon", axis=0, **self.split())

    def own_marks(self, rows):
        if self.own:
            return rows
        every = self.gather_all(rows)
        return lax.dynamic_slice_in_dim(every, self.head() * HD, HD, 0)

    def own_shard(self, block):
        if self.own:
            return block
        every = lax.all_gather(block, "lon", axis=0, tiled=True, **self.split())
        count = D // self.size
        return lax.dynamic_slice_in_dim(every, lax.axis_index("lon") * count, count, 0)

    def swap_all(self, whole):
        return lax.all_to_all(whole, "lon", 0, 0, tiled=True)

    def swap(self, keep, send):
        rows = keep.shape[0] // 8
        both = jnp.concatenate([keep, turn(send, self.core)], 1).reshape(4, 2, rows, WIDE)
        came = turn(both[:, 1], self.side)
        ready = [jnp.stack([both[k, 0], came[k]]) for k in range(4)]
        return ready[:1] + [turn(ready[4 - k], self.up[4 - k]) for k in range(1, 4)]

    def to_tokens(self, keep, send):
        if self.own:
            return self.swap(keep, send)
        part = jnp.concatenate([keep, send])
        moved = lax.all_to_all(part, "lon", 0, 0, tiled=True, **self.split())
        moved = moved.reshape(H, -1, HD)
        moved = jnp.concatenate([moved[: H // 2], moved[H // 2 :]], -1)
        return [moved[2 * k : 2 * k + 2] for k in range(4)]

    def to_heads(self, keep, send):
        rows = keep.shape[0] // 4
        if self.own:
            return [part.reshape(rows, WIDE) for part in self.swap(keep, send)]
        moved = jnp.concatenate([keep, send])
        moved = lax.all_to_all(moved, "lon", 0, 0, tiled=True, **self.split())
        moved = jnp.concatenate([moved[: keep.shape[0]], moved[keep.shape[0] :]], 1)
        return [moved[k * rows : (k + 1) * rows] for k in range(4)]

    def gather_far(self, part):
        if self.own:
            return part
        return lax.all_gather(part, "lon", axis=0, tiled=True, axis_index_groups=self.far)

    def sum_far(self, whole):
        if self.own:
            return whole
        return lax.psum_scatter(
            whole, "lon", scatter_dimension=0, tiled=True, axis_index_groups=self.far
        )

    def head(self):
        return lax.rem(lax.axis_index("lon"), H)

    def columns(self, parts):
        if not self.own:
            parts = [(self.gather_all(part), blocks) for part, blocks in parts]
        rows = parts[0][0].shape[0]
        cut = [part.reshape(rows, blocks, H, -1) for part, blocks in parts]
        if self.own:
            cut = [part.transpose(2, 0, 1, 3).reshape(H * rows, -1) for part in cut]
            return self.swap_all(jnp.concatenate(cut, 1))
        mine = [lax.dynamic_index_in_dim(part, self.head(), 2, keepdims=False) for part in cut]
        return jnp.concatenate([part.reshape(rows, -1) for part in mine], 1)

    def rows_back(self, block):
        rows, wide = block.shape[0], FF // H
        if self.own:
            moved = self.swap_all(block).reshape(H, rows // H, -1)
            expand = moved[:, :, :wide].transpose(1, 0, 2).reshape(rows // H, -1)
            attend = moved[:, :, wide:].reshape(H, rows // H, 3, HD).transpose(1, 2, 0, 3)
            return expand, attend.reshape(rows // H, -1)
        totals = []
        for part, blocks in ((block[:, :wide], 1), (block[:, wide:], 3)):
            whole = jnp.zeros((rows, blocks, H, part.shape[1] // blocks), f32)
            whole = lax.dynamic_update_index_in_dim(
                whole, part.astype(f32).reshape(rows, blocks, -1), self.head(), 2
            )
            totals.append(rounded(self.sum_all(whole.reshape(rows, -1))))
        return totals

    def own_rows(self, part):
        if self.own:
            return part
        every = self.gather_all(part)
        rows = every.shape[0] // H
        return lax.dynamic_slice_in_dim(every, self.head() * rows, rows, 0)

    def own_rows_back(self, block):
        if self.own:
            return block
        whole = jnp.zeros((block.shape[0] * H,) + block.shape[1:], f32)
        whole = lax.dynamic_update_slice_in_dim(whole, block, self.head() * block.shape[0], 0)
        return self.sum_all(whole)


def after(value, *earlier):
    return lax.optimization_barrier((value,) + earlier)[0]


def region_swap(part):
    return lax.ppermute(part, "dp", [(0, 1), (1, 0)])


def region_half(one, two, *earlier):
    is_first = lax.axis_index("dp") == 0
    keep, send = jnp.where(is_first, one, two), jnp.where(is_first, two, one)
    return rounded(keep.astype(f32) + after(region_swap(send), *earlier).astype(f32))


def region_both(part, width):
    other = region_swap(part)
    is_first = lax.axis_index("dp") == 0
    here, there = part[:, width:], other[:, width:]
    sides = [jnp.where(is_first, here, there), jnp.where(is_first, there, here)]
    return (
        part[:, :width].astype(f32) + other[:, :width].astype(f32),
        jnp.concatenate(sides, 1).astype(f32),
    )


def after_all(values, *earlier):
    return lax.optimization_barrier(tuple(values) + earlier)[: len(values)]


def quarter(blocks, k):
    return [blocks[8 * cr + 2 * k + xr] for cr in range(2) for xr in range(2)]


def region_sum(part, *earlier):
    low = rounded(part)
    if lax.axis_size("dp") == 2:
        other = after(region_swap(low), *earlier)
        return low.astype(f32) + other.astype(f32)
    return lax.psum(low, "dp").astype(f32)


def per_device(
    field,
    segment,
    padding,
    position,
    embed_weight,
    variable_embed,
    pool_query,
    pool_key,
    pool_value,
    pool_out,
    first_gain,
    first_shift,
    attend_weight,
    attend_out,
    second_gain,
    second_shift,
    expand_weight,
    expand_bias,
    reduce_weight,
    reduce_bias,
    head_weight,
    cotangent,
):
    size = lax.axis_size("lon")
    lon = Lon(size)
    rows = pool_value.shape[0]
    patch_rows, patch_cols = position.shape[0], position.shape[1]
    tokens = patch_rows * patch_cols
    many = H * tokens
    order = lon.order()

    extended = jnp.concatenate(
        [
            embed_weight.transpose(2, 1, 0).reshape(rows, PIX),
            variable_embed.T,
            jnp.zeros((rows, FULL - EXT), bf16),
        ],
        1,
    )
    pad = ((0, 0), (0, FULL - OUTW))
    seed = jnp.pad(cotangent[0].reshape(tokens, OUTW), pad)
    first = lon.first(
        jnp.concatenate([pool_value, pool_out, extended[:, :EXT]], 1),
        jnp.stack([pool_query, first_gain, first_shift, second_gain, second_shift, reduce_bias]),
        rounded(padding[0].reshape(tokens)),
    )
    second = lon.second(jnp.concatenate([attend_out, jnp.pad(head_weight, pad)], 1), seed)
    band = segment[0].reshape(1, tokens).astype(f32)
    columns = lon.columns([(attend_weight, 3), (pool_key, 1), (expand_weight, 1)])
    attend_here, expand_here = columns[:, :FULL], columns[:, FULL:]
    keyed_column = rounded(
        jnp.sum(attend_here[:, 3 * HD :].astype(f32) * lon.own_rows(pool_query).astype(f32), -1)
    )
    keyed_turned = lon.spread_columns(keyed_column)
    keyed_full = keyed_turned.T
    reduce_here = lon.own_rows(reduce_weight)
    expand_bias_here = lon.own_rows(expand_bias)

    plane = field[0]
    border = lax.ppermute(
        rounded(plane[:, 0:1, :]), "lon", [(i, (i - 1) % size) for i in range(size)]
    )
    shifted = jnp.concatenate([rounded(plane[:, 1:, :]), border], axis=1)
    pixels = (
        shifted.reshape(patch_rows, 2, patch_cols, 2, NV)
        .transpose(1, 3, 4, 0, 2)
        .reshape(PIX, tokens)
    )
    pixels = jnp.concatenate(
        [pixels, jnp.ones((NV, tokens), bf16), jnp.zeros((FULL - EXT, tokens), bf16)], 0
    ).astype(f32)

    (
        stream,
        normed_one,
        heads_turned,
        chance,
        value_rows,
        score_weight,
        vectors,
    ) = pool_forward(pixels, keyed_full, position.reshape(tokens, D), first)
    head_full = second[:, HEAD_AT:SEED_AT]
    both = rounded(mm(reduce_here, head_full))
    live = vectors[6:8].reshape(2, H, -1).transpose(1, 0, 2).reshape(H, -1)

    normed_one_all = lon.gather(normed_one)
    queries, keys, values = pack(
        order, normed_one_all, attend_here, band, live
    )
    keys_all = lon.gather_far(keys)
    values_all = lon.gather_far(values)
    out, keep, send = attend(queries, keys_all, values_all)
    heads = lon.to_tokens(keep, send)
    stream_one, normed_two = middle(
        order, second, stream, vectors, heads
    )

    normed_two_all = lon.gather(normed_two)
    grad_before, inner, bias_sums, *parts = feed(
        order,
        normed_two_all,
        expand_here,
        expand_bias_here[None],
        both,
        second,
    )
    terms, sign = lon.sum(parts)
    expand_grad = weight_grad(normed_two_all, [after(grad_before, sign)])
    bias_sums = bias_sums[0]
    grad_one, grad_branch, keep, send, sums, fields = middle_back(
        order,
        second,
        seed,
        after(stream_one, expand_grad),
        vectors,
        terms,
    )
    grad_heads = lon.to_heads(keep, send)
    early_one, early_two = early_grads(
        order, after(grad_branch, grad_heads[0]), stream_one, vectors, seed, reduce_here, inner, heads
    )
    expand_sum = rounded(region_sum(after(expand_grad, *grad_heads)))
    query_back, key_back, value_back = attend_back(
        after(queries, early_one), out, keys_all, values_all, grad_heads
    )
    key_back, value_back = lon.sum_far(key_back), lon.sum_far(value_back)
    grad_packed, *parts = unpack(
        after(query_back, expand_sum), key_back, value_back, attend_here
    )
    terms, sign = lon.sum(parts)
    early = region_half(early_one, early_two, sign)
    attend_grad = weight_grad(normed_one_all, [after(grad_packed, sign)])
    key_rows = mm(attend_here[:, 3 * HD :], first[:, 2 * D :], 0, 0)

    pixel_grad, grad_stream, *late_parts = pool_backward(
        order,
        pixels,
        score_weight,
        value_rows,
        chance,
        heads_turned,
        keyed_full,
        first,
        stream,
        grad_one,
        vectors,
        after(sums, attend_grad, key_rows),
        early,
        terms,
    )
    expand_total, attend_part = lon.rows_back(
        after(jnp.concatenate([expand_sum, attend_grad[:, : 3 * HD]], 1), *terms)
    )
    late_parts[:4] = after_all(late_parts[:4], expand_total, attend_part)
    late_terms, sign = lon.sum(late_parts, groups=False)
    attend_total = region_sum(attend_part, sign)
    late_total, early_total = region_both(
        rounded(sum(part.astype(f32) for part in late_terms)), LATE + WIDE
    )
    keyed_total = late_total[:, 2 * D + EXT : LATE]
    key_total = (keyed_total[:, :, None] * vectors[0].reshape(1, H, HD)).reshape(rows, D)
    score_total = lon.own_marks(late_total[:, LATE + 8 : LATE + 12])
    query_total = lon.own_shard(jnp.sum(key_rows * score_total.reshape(1, FULL), -1))

    grad_plane = (
        pixel_grad.reshape(2, 2, NV, patch_rows, patch_cols)
        .transpose(3, 0, 4, 1, 2)
        .reshape(2 * patch_rows, 2 * patch_cols, NV)
    )
    returned = lax.ppermute(
        rounded(after(grad_plane[:, -1:, :], sign)), "lon", [(i, (i + 1) % size) for i in range(size)]
    )
    returned = after(returned, *late_terms).astype(f32)
    field_grad = jnp.concatenate([returned, grad_plane[:, :-1, :]], axis=1)[None]

    fields = fields[:, :OUTW].reshape(1, patch_rows, patch_cols, OUTW)

    inner_total = rounded(region_sum(after(inner, sign), *late_terms))
    reduce_total = lon.own_rows_back(mm(inner_total, head_full, 1, 1))
    bias_total = region_sum(lon.own_rows_back(after(bias_sums, sign)), *late_terms)
    expand_total = expand_total.astype(f32)
    position_total = region_sum(
        after(grad_stream, sign).reshape(patch_rows, patch_cols, D), *late_terms
    )

    return (
        fields,
        field_grad,
        position_total,
        late_total[:, 2 * D : 2 * D + PIX].reshape(rows, 4, NV).transpose(2, 1, 0),
        late_total[:, 2 * D + PIX : 2 * D + EXT].T,
        query_total,
        key_total,
        late_total[:, D : 2 * D],
        late_total[:, :D],
        late_total[:, LATE],
        late_total[:, LATE + 1],
        attend_total,
        early_total[:, :D],
        late_total[:, LATE + 2],
        late_total[:, LATE + 3],
        expand_total,
        bias_total,
        reduce_total,
        late_total[:, LATE + 4],
        early_total[:, D : D + OUTW],
    )


def solution(mesh):
    in_specs = (
        P("dp", None, "lon", None),
        P("dp", None, "lon"),
        P("dp", None, "lon"),
        P(None, "lon", None),
        P(None, None, "lon"),
        P(None, "lon"),
        P("lon"),
        P("lon", None),
        P("lon", None),
        P("lon", None),
        P("lon"),
        P("lon"),
        P("lon", None),
        P("lon", None),
        P("lon"),
        P("lon"),
        P("lon", None),
        P("lon"),
        P("lon", None),
        P("lon"),
        P("lon", None),
        P("dp", None, "lon", None),
    )
    out_specs = (
        P("dp", None, "lon", None),
        P("dp", None, "lon", None),
        P(None, "lon", None),
        P(None, None, "lon"),
        P(None, "lon"),
        P("lon"),
        P("lon", None),
        P("lon", None),
        P("lon", None),
        P("lon"),
        P("lon"),
        P("lon", None),
        P("lon", None),
        P("lon"),
        P("lon"),
        P("lon", None),
        P("lon"),
        P("lon", None),
        P("lon"),
        P("lon", None),
    )
    return jax.shard_map(
        per_device, mesh=mesh, in_specs=in_specs, out_specs=out_specs, check_vma=False
    )
```

```python
import functools

import jax
import jax.numpy as jnp
from jax import lax
from jax.experimental import pallas as pl
from jax.experimental.pallas import tpu as pltpu
from jax.sharding import PartitionSpec as P

D = 1024
H = 16
HD = 64
FF = 4096
NV = 48
OUTW = 192
PIX = 4 * NV
EXT = 5 * NV
FULL = 256
LATE = 2 * D + FULL
HEAD_AT = D
SEED_AT = D + FULL
SHARE = 1
WIDE = 128
SUM_LANE = 67

EPS = 1e-05
NEGATIVE = -1e30
SCALE = HD ** (-0.5)
VMEM = 24 * 1024 * 1024
ROOMY = 56 * 1024 * 1024

f32 = jnp.float32
bf16 = jnp.bfloat16


def rounded(values):
    return values.astype(bf16)


def mm(a, b, da=1, db=0):
    return lax.dot_general(a, b, (((da,), (db,)), ((), ())), preferred_element_type=f32)


def layer_stats(values):
    center = values - jnp.mean(values, -1, keepdims=True)
    spread = lax.rsqrt(jnp.mean(center * center, -1, keepdims=True) + EPS)
    return (center * spread, spread)


def norm_back(grad_normed, normal, spread, gain):
    scaled = grad_normed * gain
    return spread * (
        scaled
        - jnp.mean(scaled, -1, keepdims=True)
        - normal * jnp.mean(scaled * normal, -1, keepdims=True)
    )


def params(limit=VMEM, **more):
    return pltpu.CompilerParams(vmem_limit_bytes=limit, **more)


SMEM_SPEC = pl.BlockSpec(memory_space=pltpu.SMEM)
WHOLE = pl.BlockSpec(memory_space=pltpu.VMEM)


def cost(flops, moved, hard=0, filler=False):
    share = 1 if filler else SHARE
    return pl.CostEstimate(flops=flops // share, bytes_accessed=moved // share, transcendentals=0)


def total(refs):
    return sum(ref[...].astype(f32) for ref in refs)


def pool_forward_kernel(
    pixels_ref,
    keyed_ref,
    position_ref,
    first_ref,
    stream_ref,
    normed_ref,
    heads_ref,
    chance_ref,
    rows_ref,
    score_ref,
    vectors_ref,
):
    pixels = pixels_ref[...]
    blank = jnp.zeros((FULL - EXT, pixels.shape[1]), f32)
    extended = first_ref[:, 2 * D :]
    last = extended[:, FULL - WIDE :].astype(f32)
    vectors_ref[...] = jnp.transpose(last)[WIDE - (FULL - EXT) :, :]
    rows_ref[...] = rounded(mm(first_ref[:, :D], extended, 0, 0))
    score_ref[...] = mm(extended, keyed_ref[...], 0, 0)
    for h in range(H):
        terms = pixels * score_ref[:, h : h + 1]
        scores = terms[:NV]
        for p in range(1, 5):
            scores = scores + terms[p * NV : (p + 1) * NV]
        scores = scores * SCALE
        raised = jnp.exp(scores - jnp.max(scores, 0, keepdims=True))
        chance = raised / jnp.sum(raised, 0, keepdims=True)
        chance_ref[h] = chance
        spread = rounded(jnp.concatenate([chance] * 5 + [blank], 0) * pixels)
        heads_ref[h * HD : (h + 1) * HD, :] = rounded(
            mm(rows_ref[h * HD : (h + 1) * HD, :], spread)
        )
    stream = mm(heads_ref[...], first_ref[:, D : 2 * D], 0, 0) + position_ref[...].astype(f32)
    stream_ref[...] = stream
    normal, unused = layer_stats(stream)
    normed_ref[...] = rounded(normal * vectors_ref[1:2, :] + vectors_ref[2:3, :])


def pool_forward(pixels, keyed, position, first):
    tokens = pixels.shape[1]
    return pl.pallas_call(
        pool_forward_kernel,
        out_shape=(
            jax.ShapeDtypeStruct((tokens, D), f32),
            jax.ShapeDtypeStruct((tokens, D), bf16),
            jax.ShapeDtypeStruct((D, tokens), bf16),
            jax.ShapeDtypeStruct((H, NV, tokens), f32),
            jax.ShapeDtypeStruct((D, FULL), bf16),
            jax.ShapeDtypeStruct((FULL, H), f32),
            jax.ShapeDtypeStruct((FULL - EXT, D), f32),
        ),
        compiler_params=params(),
        cost_estimate=cost(3_000_000_000, 8_000_000, H * NV * tokens),
        name="pool_forward",
    )(pixels, keyed, position, first)


def pool_backward_kernel(
    order_ref,
    pixels_ref,
    score_ref,
    rows_ref,
    chance_ref,
    heads_ref,
    keyed_ref,
    first_ref,
    stream_ref,
    grad_one_ref,
    vectors_ref,
    sums_ref,
    early_ref,
    other_ref,
    *refs,
):
    terms, (pixel_ref, stream_grad_ref, *outs), (late, mixed, scores, vectors) = (
        refs[: -6 - H // 2],
        refs[-6 - H // 2 : -4],
        refs[-4:],
    )
    grad_normed = total(terms)
    normal, spread = layer_stats(stream_ref[...])
    grad_stream = grad_one_ref[...] + norm_back(grad_normed, normal, spread, vectors_ref[1:2, :])
    grad_pool = rounded(grad_stream)
    stream_grad_ref[...] = grad_pool
    vectors[...] = jnp.zeros_like(vectors)
    vectors[0:1, :] = jnp.sum(grad_normed * normal, 0, keepdims=True)
    vectors[1:2, :] = jnp.sum(grad_normed, 0, keepdims=True)
    vectors[2:5, :] = sums_ref[0:3, :]
    grad_heads = rounded(mm(first_ref[:, D : 2 * D], grad_pool, 1, 1))
    late[:, :D] = rounded(mm(heads_ref[...], grad_pool))

    pixels = pixels_ref[...]
    tokens = pixels.shape[1]
    blank = jnp.zeros((FULL - EXT, tokens), f32)
    pixel_ref[...] = jnp.zeros_like(pixel_ref)
    scores[...] = jnp.zeros_like(scores)
    late[:, LATE:] = rounded(jnp.transpose(vectors[...]))
    fours = lax.broadcasted_iota(jnp.int32, (HD, FULL), 1) // 4
    fours = rounded(fours == lax.broadcasted_iota(jnp.int32, (HD, FULL), 0))
    lane = lax.broadcasted_iota(jnp.int32, (FULL, WIDE), 1) - 8
    within = lane == lax.broadcasted_iota(jnp.int32, (FULL, WIDE), 0) % 4
    for h in range(H):
        block = slice(h * HD, (h + 1) * HD)
        grad = grad_heads[block, :]
        chance = chance_ref[h]
        wide = jnp.concatenate([chance] * 5 + [blank], 0)
        back = mm(rows_ref[block, :], grad, 0, 0)
        parts = back * pixels
        grad_chance = parts[:NV]
        for p in range(1, 5):
            grad_chance = grad_chance + parts[p * NV : (p + 1) * NV]
        grad_score = chance * (grad_chance - jnp.sum(chance * grad_chance, 0, keepdims=True))
        grad_wide = jnp.concatenate([grad_score * SCALE] * 5 + [blank], 0)
        mixed[block, :] = rounded(mm(grad, rounded(wide * pixels), 1, 1))
        score_grad = jnp.sum(grad_wide * pixels, 1, keepdims=True)
        scores[:, h : h + 1] = score_grad
        late[block, LATE:] += rounded(mm(fours, rounded(jnp.where(within, score_grad, 0.0))))
        pixel_ref[...] += (
            wide[:PIX] * back[:PIX] + grad_wide[:PIX] * score_ref[:PIX, h : h + 1]
        )
    score_grads = rounded(scores[:, :H])
    extended = first_ref[:, 2 * D :]
    late[:, D : 2 * D] = rounded(mm(extended, mixed[...], 1, 1))
    embed_grad = mm(first_ref[:, :D], mixed[...]) + mm(keyed_ref[...], score_grads, 1, 1)
    keyed_grad = mm(extended, score_grads)
    last = jnp.concatenate([keyed_grad, jnp.zeros((D, FULL - H), f32)], 1)
    late[:, 2 * D : LATE] = rounded(
        jnp.where(
            lax.broadcasted_iota(jnp.int32, embed_grad.shape, 1) < EXT,
            embed_grad,
            pltpu.roll(last, EXT, 1),
        )
    )
    for i, ref in enumerate(outs):
        for j in range(2):
            start = pl.multiple_of(order_ref[2 * i + j] * HD, HD)
            ref[j * HD : (j + 1) * HD, : LATE + WIDE] = late[pl.ds(start, HD), :]
        block = slice(2 * i * HD, (2 * i + 2) * HD)
        ref[:, LATE + WIDE :] = rounded(
            early_ref[block, :].astype(f32) + other_ref[block, :].astype(f32)
        )


def pool_backward(
    order, pixels, score, rows, chance, heads, keyed, first, stream, grad_one, vectors, sums, early, other, terms
):
    tokens = pixels.shape[1]
    return pl.pallas_call(
        pool_backward_kernel,
        in_specs=[SMEM_SPEC] + [WHOLE] * (13 + len(terms)),
        out_shape=[
            jax.ShapeDtypeStruct((PIX, tokens), f32),
            jax.ShapeDtypeStruct((tokens, D), bf16),
        ]
        + [jax.ShapeDtypeStruct((2 * HD, LATE + WIDE + early.shape[1]), bf16)] * (H // 2),
        scratch_shapes=[
            pltpu.VMEM((D, LATE + WIDE), bf16),
            pltpu.VMEM((D, FULL), bf16),
            pltpu.VMEM((FULL, WIDE), f32),
            pltpu.VMEM((WIDE, D), f32),
        ],
        compiler_params=params(ROOMY),
        cost_estimate=cost(4_000_000_000, 14_000_000),
        name="pool_backward",
    )(
        order,
        pixels,
        score,
        rows,
        chance,
        heads,
        keyed,
        first,
        stream,
        grad_one,
        vectors,
        sums,
        early,
        other,
        *terms,
    )


def finish_kernel(
    first_ref,
    low_ref,
    other_ref,
    vectors_ref,
    key_ref,
    pool_ref,
    value_ref,
    embed_ref,
    key_grad_ref,
    out_ref,
    head_ref,
    variable_ref,
    *mark_refs,
):
    low, other = low_ref[...].astype(f32), other_ref[...].astype(f32)
    rows = low.shape[0]
    both = low[:, : LATE + WIDE] + other[:, : LATE + WIDE]
    pool_ref[...] = both[:, :D]
    value_ref[...] = both[:, D : 2 * D]
    last = both[:, 2 * D : LATE]
    turned = jnp.transpose(last)
    for p in range(4):
        embed_ref[:, p, :] = turned[p * NV : (p + 1) * NV]
    variable_ref[...] = turned[PIX:EXT]
    lane = lax.broadcasted_iota(jnp.int32, (H, D), 1) // HD
    spread = (lane == lax.broadcasted_iota(jnp.int32, (H, D), 0)).astype(f32)
    key_grad_ref[...] = (
        jnp.dot(
            last[:, EXT:],
            spread,
            precision=lax.Precision.HIGHEST,
            preferred_element_type=f32,
        )
        * vectors_ref[0:1, :]
    )
    marks = both[:, LATE:]
    column = lax.broadcasted_iota(jnp.int32, (rows, FULL), 1)
    scores = jnp.zeros((rows, FULL), f32)
    for c in range(4):
        scores = jnp.where(column % 4 == c, marks[:, 8 + c : 9 + c], scores)
    row = lax.broadcasted_iota(jnp.int32, (rows, FULL), 0)
    scores = jnp.sum(jnp.where(column // 4 == row, scores, 0.0), 0, keepdims=True)
    query = jnp.sum(key_ref[...] * scores, 1, keepdims=True)
    lane = lax.broadcasted_iota(jnp.int32, (rows, WIDE), 1)
    marks = jnp.transpose(jnp.where(lane == 5, query, marks))
    for i, ref in enumerate(mark_refs):
        ref[...] = marks[i : i + 1]
    here, there = low[:, LATE + WIDE :], other[:, LATE + WIDE :]
    is_first = first_ref[0] == 1
    left = jnp.where(is_first, here, there)
    right = jnp.where(is_first, there, here)
    half = left.shape[1]
    out_ref[:, :half] = left
    out_ref[:, half:] = right[:, : D - half]
    head_ref[...] = right[:, D - half : D - half + OUTW]


def finish(is_first, low, other, vectors, key_rows):
    rows = low.shape[0]
    wide = jax.ShapeDtypeStruct((rows, D), f32)
    return pl.pallas_call(
        finish_kernel,
        in_specs=[SMEM_SPEC] + [WHOLE] * 4,
        out_shape=(
            wide,
            wide,
            jax.ShapeDtypeStruct((NV, 4, rows), f32),
            wide,
            wide,
            jax.ShapeDtypeStruct((rows, OUTW), f32),
            jax.ShapeDtypeStruct((NV, rows), f32),
        )
        + (jax.ShapeDtypeStruct((1, rows), f32),) * 6,
        compiler_params=params(),
        cost_estimate=cost(4 * H * D * rows, 3_000_000),
        name="finish",
    )(is_first, low, other, vectors, key_rows)


def copy_parts(refs, into):
    start = 0
    for ref in refs:
        into[start : start + ref.shape[0], :] = ref[...]
        start += ref.shape[0]


def columns_from(rows):
    width = rows[0].shape[1]
    return jnp.concatenate(
        [jnp.transpose(jnp.broadcast_to(row, (width, width))) for row in rows], 0
    )


def pack_kernel(table_ref, weight_ref, band_ref, live_ref, *refs):
    parts, (query_ref, key_ref, value_ref, every) = refs[:-4], refs[-4:]
    copy_parts(parts, every)
    count = every.shape[0]
    block = 512
    blocks = H * block // count
    for i in range(count // block):
        rows = slice(i * block, (i + 1) * block)
        packed = rounded(mm(every[rows, :], weight_ref[...])).astype(f32)
        here = range(i * blocks, (i + 1) * blocks)
        live = columns_from([live_ref[pl.ds(table_ref[e], 1), :] for e in here])
        band = columns_from([band_ref[...]] * blocks)
        left, right = packed[:, :WIDE], packed[:, WIDE:]
        lane = lax.broadcasted_iota(jnp.int32, left.shape, 1)
        query = jnp.where(lane == HD, 1.0 - band, jnp.where(lane == HD + 1, band, 0.0))
        query_ref[rows, :] = rounded(jnp.where(lane < HD, left * SCALE, query))
        key = jnp.where(
            lane == HD,
            NEGATIVE * (1.0 - live * (1.0 - band)),
            jnp.where(
                lane == HD + 1,
                NEGATIVE * (1.0 - live * band),
                jnp.where(lane < HD + 5, -1.0, 0.0),
            ),
        )
        key_ref[rows, :] = rounded(jnp.where(lane < HD, pltpu.roll(left, HD, 1), key))
        value = jnp.where(lane < SUM_LANE, -1.0, jnp.where(lane == SUM_LANE, 1.0, 0.0))
        value_ref[rows, :] = rounded(jnp.where(lane < HD, right, value))


def pack(table, parts, weight, band, live):
    count = sum(part.shape[0] for part in parts)
    return pl.pallas_call(
        pack_kernel,
        in_specs=[SMEM_SPEC] + [WHOLE] * (3 + len(parts)),
        out_shape=[jax.ShapeDtypeStruct((count, WIDE), bf16)] * 3,
        scratch_shapes=[pltpu.VMEM((count, D), bf16)],
        compiler_params=params(),
        cost_estimate=cost(2 * count * D * FULL, 3 * count * D),
        name="pack",
    )(table, weight, band, live, *parts)


def attend_kernel(query_ref, key_ref, value_ref, out_ref, keep_ref, send_ref, *, half):
    scores = mm(query_ref[...], key_ref[...], 1, 1)
    summit = jnp.max(scores, -1, keepdims=True)
    raised = rounded(jnp.exp(scores - summit))
    total = mm(raised, value_ref[...])
    amount = total[:, SUM_LANE : SUM_LANE + 1]
    lane = lax.broadcasted_iota(jnp.int32, total.shape, 1)
    out = jnp.where(lane < HD, total / amount, summit + jnp.log(amount))
    out_ref[...] = out
    low = rounded(out[:, :HD])

    @pl.when(pl.program_id(0) < half)
    def _():
        keep_ref[...] = low

    @pl.when(pl.program_id(0) >= half)
    def _():
        send_ref[...] = low


def attend(queries, keys, values):
    rows, count = queries.shape[0], keys.shape[0]
    block = min(256, max(32, 256 * 2048 // count))
    half = rows // block // 2
    return pl.pallas_call(
        functools.partial(attend_kernel, half=half),
        grid=(2 * half,),
        in_specs=[
            pl.BlockSpec((block, WIDE), lambda i: (i, 0)),
            pl.BlockSpec((count, WIDE), lambda i: (0, 0)),
            pl.BlockSpec((count, WIDE), lambda i: (0, 0)),
        ],
        out_specs=(
            pl.BlockSpec((block, WIDE), lambda i: (i, 0)),
            pl.BlockSpec((block, HD), lambda i: (jnp.minimum(i, half - 1), 0)),
            pl.BlockSpec((block, HD), lambda i: (jnp.maximum(i - half, 0), 0)),
        ),
        out_shape=(
            jax.ShapeDtypeStruct((rows, WIDE), f32),
            jax.ShapeDtypeStruct((rows // 2, HD), bf16),
            jax.ShapeDtypeStruct((rows // 2, HD), bf16),
        ),
        compiler_params=params(dimension_semantics=("arbitrary",)),
        cost_estimate=cost(4 * rows * count * WIDE, rows * WIDE * 6 + count * WIDE * 4),
        name="attend",
    )(queries, keys, values)


def three_parts(values):
    high = rounded(values)
    rest = values - high.astype(f32)
    middle = rounded(rest)
    low = rounded(rest - middle.astype(f32))
    return [part.astype(f32) for part in (high, middle, low)]


def attend_back_kernel(
    query_ref,
    out_ref,
    key_ref,
    value_ref,
    *refs,
):
    moved_refs, (query_grad_ref, key_grad_ref, value_grad_ref, queries, grads) = (
        refs[:-5],
        refs[-5:],
    )

    @pl.when(pl.program_id(0) == 0)
    def _():
        lane = lax.broadcasted_iota(jnp.int32, queries.shape, 1)
        out = out_ref[...]
        log_total = out[:, HD : HD + 1]
        moved = jnp.concatenate([ref[...] for ref in moved_refs], 0).astype(f32)
        grad = jnp.concatenate([moved, pltpu.roll(moved, HD, 1)], 0)
        grad = jnp.where(lane < HD, grad, 0.0)
        balance = jnp.sum(out * grad, -1, keepdims=True)
        query = query_ref[...].astype(f32)
        for i, part in enumerate(three_parts(log_total)):
            query = jnp.where(lane == HD + 2 + i, part, query)
        for i, part in enumerate(three_parts(balance)):
            grad = jnp.where(lane == HD + i, part, grad)
        queries[...] = rounded(query)
        grads[...] = rounded(grad)
        query_grad_ref[...] = jnp.zeros_like(query_grad_ref)

    prob = jnp.exp(mm(key_ref[...], queries[...], 1, 1))
    slope = mm(value_ref[...], grads[...], 1, 1)
    grad_scores = rounded(prob * slope)
    value_grad_ref[...] = mm(rounded(prob), grads[...])
    key_grad_ref[...] = mm(grad_scores, queries[...])
    query_grad_ref[...] += mm(key_ref[...], grad_scores, 0, 0)


def attend_back(queries, out, keys, values, moved):
    rows, count = queries.shape[0], keys.shape[0]
    block = 512
    whole = pl.BlockSpec((rows, WIDE), lambda i: (0, 0))
    part = pl.BlockSpec((block, WIDE), lambda i: (i, 0))
    return pl.pallas_call(
        attend_back_kernel,
        grid=(count // block,),
        in_specs=[
            whole,
            whole,
            part,
            part,
        ]
        + [WHOLE] * len(moved),
        out_specs=(pl.BlockSpec((WIDE, rows), lambda i: (0, 0)), part, part),
        out_shape=(
            jax.ShapeDtypeStruct((WIDE, rows), f32),
            jax.ShapeDtypeStruct((count, WIDE), f32),
            jax.ShapeDtypeStruct((count, WIDE), f32),
        ),
        scratch_shapes=[pltpu.VMEM((rows, WIDE), bf16), pltpu.VMEM((rows, WIDE), bf16)],
        compiler_params=params(dimension_semantics=("arbitrary",)),
        cost_estimate=cost(10 * rows * count * WIDE, rows * WIDE * 12 + count * WIDE * 14),
        name="attend_back",
    )(queries, out, keys, values, *moved)


def unpack_kernel(query_ref, key_ref, value_ref, weight_ref, packed_ref, *refs):
    weight = weight_ref[...]
    step = key_ref.shape[0] // len(refs)
    for i, ref in enumerate(refs):
        rows = slice(i * step, (i + 1) * step)
        query = jnp.transpose(query_ref[:, rows]) * SCALE
        lane = lax.broadcasted_iota(jnp.int32, (step, WIDE), 1)
        left = jnp.where(lane < HD, query, pltpu.roll(key_ref[rows, :], HD, 1))
        right = jnp.where(lane < HD, value_ref[rows, :], 0.0)
        packed = rounded(jnp.concatenate([left, right], 1))
        packed_ref[rows, :] = packed
        ref[...] = rounded(mm(packed, weight, 1, 1))


def unpack(query_back, key_back, value_back, weight):
    count = key_back.shape[0]
    return pl.pallas_call(
        unpack_kernel,
        out_shape=[jax.ShapeDtypeStruct((count, FULL), bf16)]
        + [jax.ShapeDtypeStruct((count // 8, D), bf16)] * 8,
        compiler_params=params(),
        cost_estimate=cost(2 * count * D * FULL, 4 * count * D),
        name="unpack",
    )(query_back, key_back, value_back, weight)


def weight_grad_kernel(beside_ref, *refs, count, width):
    parts, grads, (out_ref, every, changes) = refs[:count], refs[count:-3], refs[-3:]
    left = beside_ref.shape[1] if width else 0
    if left:
        out_ref[:, :left] = beside_ref[...]
    copy_parts(parts, every)
    copy_parts(grads, changes)
    block = 256
    for i in range(D // block):
        columns = slice(i * block, (i + 1) * block)
        grad = rounded(mm(every[:, columns], changes[...], 0, 0))
        out_ref[columns, left:] = grad[:, : out_ref.shape[1] - left]


def weight_grad(parts, grads, beside=None, keep=None):
    count, width = sum(grad.shape[0] for grad in grads), grads[0].shape[1]
    wide = width if beside is None else beside.shape[1] + keep
    return pl.pallas_call(
        functools.partial(
            weight_grad_kernel, count=len(parts), width=0 if beside is None else keep
        ),
        out_shape=jax.ShapeDtypeStruct((D, wide), bf16),
        scratch_shapes=[pltpu.VMEM((count, D), bf16), pltpu.VMEM((count, width), bf16)],
        compiler_params=params(),
        cost_estimate=cost(20 * count * D * width, 3 * count * D, filler=True),
        name="weight_grad",
    )(grads[0] if beside is None else beside, *parts, *grads)


def sort_rows(order_ref, from_ref, into):
    for i in range(H):
        start = pl.multiple_of(order_ref[(i % 2) * 8 + i // 2] * HD, HD)
        into[i * HD : (i + 1) * HD, :] = from_ref[pl.ds(start, HD), :D]


def heads_of(refs):
    return jnp.concatenate([ref[i] for ref in refs for i in range(2)], 1)


def middle_kernel(order_ref, second_ref, stream_ref, vectors_ref, *refs):
    heads, (one_ref, normed_ref, sorted_w) = refs[:-3], refs[-3:]
    sort_rows(order_ref, second_ref, sorted_w)
    stream = stream_ref[...] + mm(heads_of(heads), sorted_w[...])
    one_ref[...] = stream
    normal, unused = layer_stats(stream)
    normed_ref[...] = rounded(normal * vectors_ref[3:4, :] + vectors_ref[4:5, :])


def middle(order, second, stream, vectors, heads):
    tokens = stream.shape[0]
    return pl.pallas_call(
        middle_kernel,
        in_specs=[SMEM_SPEC] + [WHOLE] * (3 + len(heads)),
        out_shape=(
            jax.ShapeDtypeStruct((tokens, D), f32),
            jax.ShapeDtypeStruct((tokens, D), bf16),
        ),
        scratch_shapes=[pltpu.VMEM((D, D), bf16)],
        compiler_params=params(),
        cost_estimate=cost(2 * tokens * D * D, 2 * D * D + 12 * tokens * D),
        name="middle",
    )(order, second, stream, vectors, *heads)


def middle_back_kernel(order_ref, second_ref, seed_ref, stream_ref, vectors_ref, *refs):
    terms, (one_ref, branch_ref, keep_ref, send_ref, sums_ref, fields_ref, sorted_w) = (
        refs[:-7],
        refs[-7:],
    )
    sort_rows(order_ref, second_ref, sorted_w)
    summed = total(terms)
    head = second_ref[:, HEAD_AT:SEED_AT]
    grad_normed = summed[:, :D]
    fields_ref[...] = summed[:, D:] + mm(rounded(stream_ref[...] + vectors_ref[5:6, :]), head)
    stream = stream_ref[...]
    grad_two = rounded(mm(seed_ref[...], head, 1, 1)).astype(f32)
    normal, spread = layer_stats(stream)
    grad_one = grad_two + norm_back(grad_normed, normal, spread, vectors_ref[3:4, :])
    one_ref[...] = grad_one
    branch = rounded(grad_one)
    branch_ref[...] = branch
    back = rounded(mm(branch, sorted_w[...], 1, 1)).astype(f32)
    tokens = stream.shape[0]
    for i in range(H // 2):
        pair = back[:, i * WIDE : (i + 1) * WIDE]
        rows = slice(i * tokens, (i + 1) * tokens)
        keep_ref[rows, :] = rounded(pair[:, :HD])
        send_ref[rows, :] = rounded(pltpu.roll(pair, HD, 1)[:, :HD])
    sums_ref[...] = jnp.zeros_like(sums_ref)
    sums_ref[0:1, :] = jnp.sum(grad_normed * normal, 0, keepdims=True)
    sums_ref[1:2, :] = jnp.sum(grad_normed, 0, keepdims=True)
    sums_ref[2:3, :] = jnp.sum(grad_two, 0, keepdims=True)


def middle_back(order, second, seed, stream, vectors, terms):
    tokens = stream.shape[0]
    half = H // 2 * tokens
    return pl.pallas_call(
        middle_back_kernel,
        in_specs=[SMEM_SPEC] + [WHOLE] * (4 + len(terms)),
        out_shape=(
            jax.ShapeDtypeStruct((tokens, D), f32),
            jax.ShapeDtypeStruct((tokens, D), bf16),
            jax.ShapeDtypeStruct((half, HD), bf16),
            jax.ShapeDtypeStruct((half, HD), bf16),
            jax.ShapeDtypeStruct((8, D), f32),
            jax.ShapeDtypeStruct((tokens, FULL), f32),
        ),
        scratch_shapes=[pltpu.VMEM((D, D), bf16)],
        compiler_params=params(),
        cost_estimate=cost(3 * tokens * D * D, 3 * D * D + 20 * tokens * D),
        name="middle_back",
    )(order, second, seed, stream, vectors, *terms)


def early_kernel(
    order_ref, first_ref, branch_ref, stream_ref, vectors_ref, seed_ref, reduce_ref, inner_ref, *refs
):
    heads, (keep_ref, send_ref, rows) = refs[:-3], refs[-3:]
    branch = branch_ref[...]
    half = keep_ref.shape[1]
    is_first = first_ref[0] == 1
    stream = rounded(stream_ref[...] + vectors_ref[5:6, :])
    rows[...] = mm(stream, seed_ref[...], 0, 0) + mm(reduce_ref[...], inner_ref[...], 0, 0)
    for i in range(H // 2):
        pair = mm(heads[i // 2][i % 2], branch, 0, 0)
        for j in range(2):
            e = j * 8 + i
            start = pl.multiple_of(order_ref[e] * HD, HD)
            here = pair[j * HD : (j + 1) * HD]
            one = here[:, :half]
            two = jnp.concatenate([here[:, half:], rows[pl.ds(start, HD), :]], 1)
            block = slice(e * HD, (e + 1) * HD)
            keep_ref[block, :] = rounded(jnp.where(is_first, one, two))
            send_ref[block, :] = rounded(jnp.where(is_first, two, one))


def early_grads(order, is_first, branch, stream, vectors, seed, reduce_here, inner, heads):
    tokens = stream.shape[0]
    half = (D + FULL) // 2
    return pl.pallas_call(
        early_kernel,
        in_specs=[SMEM_SPEC] * 2 + [WHOLE] * (6 + len(heads)),
        out_shape=(
            jax.ShapeDtypeStruct((D, half), bf16),
            jax.ShapeDtypeStruct((D, half), bf16),
        ),
        scratch_shapes=[pltpu.VMEM((D, FULL), f32)],
        compiler_params=params(),
        cost_estimate=cost(20 * tokens * D * (D + FULL), 6_000_000, filler=True),
        name="early_grads",
    )(order, is_first, branch, stream, vectors, seed, reduce_here, inner, *heads)


def feed_kernel(order_ref, expand_ref, bias_ref, both_ref, second_ref, *refs):
    parts, (before_ref, inner_ref, sums_ref, *outs) = refs[:H], refs[H:]
    expand = expand_ref[...]
    both = both_ref[...]
    inner = jnp.zeros(inner_ref.shape, f32)
    sums = jnp.zeros((1, expand.shape[1]), f32)
    tokens = parts[0].shape[0]
    step = 2 * tokens
    for i in range(8):
        block = slice(i * step, (i + 1) * step)
        rows = jnp.concatenate([parts[2 * i][...], parts[2 * i + 1][...]], 0)
        before = mm(rows, expand) + bias_ref[...].astype(f32)
        half = 0.5 + 0.5 * lax.erf(before * 0.7071067811865476)
        hidden = rounded(before * half)
        slope = half + before * jnp.exp(-0.5 * before * before) * 0.3989422804014327
        seed = jnp.concatenate(
            [
                second_ref[pl.ds(pl.multiple_of(order_ref[e] * HD, HD), HD), at : at + FULL]
                for e in (2 * i, 2 * i + 1)
                for at in (SEED_AT, SEED_AT + FULL)
            ],
            0,
        )
        grad = rounded(mm(seed, both, 1, 1) * slope)
        before_ref[block, :] = grad
        outs[i][:, :D] = rounded(mm(grad, expand, 1, 1))
        outs[i][:, D:] = rounded(mm(hidden, both))
        inner = inner + mm(hidden, seed, 0, 0)
        sums = sums + jnp.sum(grad.astype(f32), 0, keepdims=True)
    inner_ref[...] = rounded(inner)
    sums_ref[...] = jnp.broadcast_to(sums, sums_ref.shape)


def feed(order, parts, expand, bias, both, second):
    tokens = parts[0].shape[0]
    count, width = H * tokens, expand.shape[1]
    return pl.pallas_call(
        feed_kernel,
        in_specs=[SMEM_SPEC] + [WHOLE] * (4 + H),
        out_shape=[
            jax.ShapeDtypeStruct((count, width), bf16),
            jax.ShapeDtypeStruct((width, FULL), bf16),
            jax.ShapeDtypeStruct((8, width), f32),
        ]
        + [jax.ShapeDtypeStruct((2 * tokens, D + FULL), bf16)] * 8,
        compiler_params=params(),
        cost_estimate=cost(6 * count * D * width, 5 * count * D),
        name="feed",
    )(order, expand, bias, both, second, *parts)


def turn(array, pairs):
    return lax.ppermute(array, "lon", pairs)


class Steps:
    def __init__(self, lon, ready):
        self.lon, self.ready = lon, ready
        self.side, self.mine, self.low, self.sent = {}, {}, {}, {}

    def add(self, k, keep, send):
        rows = keep.shape[0] // 2
        came = turn(send, self.lon.core)
        away = rounded(keep[rows:].astype(f32) + came[rows:].astype(f32))
        if k in (3, 0):
            away = after(away, self.low[2], *self.ready)
        self.side[k] = turn(away, self.lon.side)
        self.mine[k] = (
            keep[:rows].astype(f32) + came[:rows].astype(f32) + self.side[k].astype(f32)
        )
        if k:
            self.low[k] = rounded(self.mine[k])
            self.sent[k] = turn(self.low[k], self.lon.up[k])

    def terms(self):
        return [self.mine[0], self.sent[1], self.sent[2], self.sent[3]]


class Lon:
    def __init__(self, size):
        self.size = size
        self.groups = size // H
        self.near = [[g * H + h for h in range(H)] for g in range(self.groups)]
        self.far = [[g * H + h for g in range(self.groups)] for h in range(H)]
        self.own = self.groups == 1
        every = range(H)
        self.core = [(i, i ^ 1) for i in every]
        self.side = [(i, i ^ 2) for i in every]
        self.down = [[(i, (i + 4 * k) % H) for i in every] for k in range(4)]
        self.up = [[(i, (i - 4 * k) % H) for i in every] for k in range(4)]

    def split(self):
        return {"axis_index_groups": self.near}

    def order(self):
        if not self.own:
            return jnp.arange(H, dtype=jnp.int32)
        here = lax.axis_index("lon")
        z, x, core = here // 4, (here // 2) % 2, here % 2
        return jnp.stack(
            [
                ((z - k) % 4) * 4 + (x ^ xr) * 2 + (core ^ cr)
                for cr in range(2)
                for k in range(4)
                for xr in range(2)
            ]
        ).astype(jnp.int32)

    def gather_all(self, part):
        return lax.all_gather(part, "lon", axis=0, tiled=True)

    def sum_all(self, whole):
        return lax.psum_scatter(whole, "lon", scatter_dimension=0, tiled=True)

    def gather(self, part, groups=True, ready=()):
        if not self.own:
            split = self.split() if groups else {}
            whole = lax.all_gather(part, "lon", axis=0, tiled=True, **split)
            rows = whole.shape[0] // H
            return [whole[i * rows : (i + 1) * rows] for i in range(H)]
        line = {0: part, 1: turn(part, self.down[1]), 3: turn(part, self.down[3])}
        side = {0: turn(part, self.side)}
        line[2] = turn(after(part, line[1], line[3], *ready), self.down[2])
        for k in (1, 3, 2):
            side[k] = turn(line[k], self.side)
        mine = [piece for k in range(4) for piece in (line[k], side[k])]
        return mine + [turn(piece, self.core) for piece in mine]

    def gather_group(self, part):
        return lax.all_gather(part, "lon", axis=0, tiled=True, **({} if self.own else self.split()))

    def sum(self, parts, groups=True, ready=()):
        if not self.own:
            whole = jnp.concatenate(parts)
            split = self.split() if groups else {}
            whole = lax.psum_scatter(whole, "lon", scatter_dimension=0, tiled=True, **split)
            return [whole], whole
        steps = Steps(self, ready)
        for k in (2, 1, 3, 0):
            steps.add(k, parts[k], parts[4 + k])
        return steps.terms(), steps.side[0]

    def first(self, weights, vectors, live):
        spare = FULL - EXT
        if not self.own:
            vectors = lax.all_gather(vectors, "lon", axis=1, tiled=True)
            live = self.gather_group(live).reshape(H, 2, HD).transpose(1, 0, 2)
        marks = jnp.concatenate([vectors, live.reshape(2, -1)]).T
        marks = jnp.pad(marks, ((0, 0), (0, spare - marks.shape[1])))
        if not self.own:
            return jnp.concatenate([self.gather_all(weights), marks], 1)
        return self.gather_all(jnp.concatenate([weights, marks], 1))

    def second(self, weights, seed):
        if not self.own:
            seed = self.gather_group(seed).reshape(H, 2, HD, FULL).transpose(0, 2, 1, 3)
            return jnp.concatenate([self.gather_all(weights), seed.reshape(D, 2 * FULL)], 1)
        half = seed.shape[0] // 2
        return self.gather_all(jnp.concatenate([weights, seed[:half], seed[half:]], 1))

    def spread_columns(self, column):
        if self.own:
            return self.swap_all(jnp.tile(column[None], (H, 1)))
        return lax.all_gather(column, "lon", axis=0, **self.split())

    def own_marks(self, rows):
        if self.own:
            return rows
        every = self.gather_all(rows)
        return lax.dynamic_slice_in_dim(every, self.head() * HD, HD, 0)

    def own_shard(self, block):
        if self.own:
            return block
        every = lax.all_gather(block, "lon", axis=0, tiled=True, **self.split())
        count = D // self.size
        return lax.dynamic_slice_in_dim(every, lax.axis_index("lon") * count, count, 0)

    def swap_all(self, whole):
        return lax.all_to_all(whole, "lon", 0, 0, tiled=True)

    def swap(self, keep, send):
        rows = keep.shape[0] // 8
        both = jnp.concatenate([keep, turn(send, self.core)], 1).reshape(4, 2, rows, WIDE)
        came = turn(both[:, 1], self.side)
        ready = [jnp.stack([both[k, 0], came[k]]) for k in range(4)]
        return ready[:1] + [turn(ready[4 - k], self.up[4 - k]) for k in range(1, 4)]

    def to_tokens(self, keep, send):
        if self.own:
            return self.swap(keep, send)
        part = jnp.concatenate([keep, send])
        moved = lax.all_to_all(part, "lon", 0, 0, tiled=True, **self.split())
        moved = moved.reshape(H, -1, HD)
        moved = jnp.concatenate([moved[: H // 2], moved[H // 2 :]], -1)
        return [moved[2 * k : 2 * k + 2] for k in range(4)]

    def to_heads(self, keep, send):
        rows = keep.shape[0] // 4
        if self.own:
            return [part.reshape(rows, WIDE) for part in self.swap(keep, send)]
        moved = jnp.concatenate([keep, send])
        moved = lax.all_to_all(moved, "lon", 0, 0, tiled=True, **self.split())
        moved = jnp.concatenate([moved[: keep.shape[0]], moved[keep.shape[0] :]], 1)
        return [moved[k * rows : (k + 1) * rows] for k in range(4)]

    def gather_far(self, part):
        if self.own:
            return part
        return lax.all_gather(part, "lon", axis=0, tiled=True, axis_index_groups=self.far)

    def sum_far(self, whole):
        if self.own:
            return whole
        return lax.psum_scatter(
            whole, "lon", scatter_dimension=0, tiled=True, axis_index_groups=self.far
        )

    def head(self):
        return lax.rem(lax.axis_index("lon"), H)

    def columns(self, parts):
        if not self.own:
            parts = [(self.gather_all(part), blocks) for part, blocks in parts]
        rows = parts[0][0].shape[0]
        cut = [part.reshape(rows, blocks, H, -1) for part, blocks in parts]
        if self.own:
            cut = [part.transpose(2, 0, 1, 3).reshape(H * rows, -1) for part in cut]
            return self.swap_all(jnp.concatenate(cut, 1))
        mine = [lax.dynamic_index_in_dim(part, self.head(), 2, keepdims=False) for part in cut]
        return jnp.concatenate([part.reshape(rows, -1) for part in mine], 1)

    def rows_back(self, block):
        if self.own:
            return [self.swap_all(block)]
        rows, wide = block.shape[0], FF // H
        totals = []
        for part, blocks in ((block[:, :wide], 1), (block[:, wide:], 3)):
            whole = jnp.zeros((rows, blocks, H, part.shape[1] // blocks), f32)
            whole = lax.dynamic_update_index_in_dim(
                whole, part.astype(f32).reshape(rows, blocks, -1), self.head(), 2
            )
            totals.append(rounded(self.sum_all(whole.reshape(rows, -1))))
        return totals

    def shards(self, moved):
        if not self.own:
            return moved
        wide = FF // H
        moved = moved[0].reshape(H, -1, moved[0].shape[1])
        rows = moved.shape[1]
        expand = moved[:, :, :wide].transpose(1, 0, 2).reshape(rows, -1)
        attend = moved[:, :, wide:].reshape(H, rows, 3, HD).transpose(1, 2, 0, 3)
        return [expand, attend.reshape(rows, -1)]

    def own_rows(self, part):
        if self.own:
            return part
        every = self.gather_all(part)
        rows = every.shape[0] // H
        return lax.dynamic_slice_in_dim(every, self.head() * rows, rows, 0)

    def own_rows_back(self, block):
        if self.own:
            return block
        whole = jnp.zeros((block.shape[0] * H,) + block.shape[1:], f32)
        whole = lax.dynamic_update_slice_in_dim(whole, block, self.head() * block.shape[0], 0)
        return self.sum_all(whole)


def after(value, *earlier):
    return lax.optimization_barrier((value,) + earlier)[0]


def region_swap(part):
    return lax.ppermute(part, "dp", [(0, 1), (1, 0)])


def region_both(part, width):
    other = region_swap(part)
    is_first = lax.axis_index("dp") == 0
    here, there = part[:, width:], other[:, width:]
    sides = [jnp.where(is_first, here, there), jnp.where(is_first, there, here)]
    return (
        part[:, :width].astype(f32) + other[:, :width].astype(f32),
        jnp.concatenate(sides, 1).astype(f32),
    )


def after_all(values, *earlier):
    return lax.optimization_barrier(tuple(values) + earlier)[: len(values)]


def quarter(blocks, k):
    return [blocks[8 * cr + 2 * k + xr] for cr in range(2) for xr in range(2)]


def region_sum(part, *earlier):
    low = rounded(part)
    if lax.axis_size("dp") == 2:
        other = after(region_swap(low), *earlier)
        return low.astype(f32) + other.astype(f32)
    return lax.psum(low, "dp").astype(f32)


def per_device(
    field,
    segment,
    padding,
    position,
    embed_weight,
    variable_embed,
    pool_query,
    pool_key,
    pool_value,
    pool_out,
    first_gain,
    first_shift,
    attend_weight,
    attend_out,
    second_gain,
    second_shift,
    expand_weight,
    expand_bias,
    reduce_weight,
    reduce_bias,
    head_weight,
    cotangent,
):
    size = lax.axis_size("lon")
    lon = Lon(size)
    rows = pool_value.shape[0]
    patch_rows, patch_cols = position.shape[0], position.shape[1]
    tokens = patch_rows * patch_cols
    many = H * tokens
    order = lon.order()
    is_first = (lax.axis_index("dp") == 0).astype(jnp.int32).reshape(1)

    extended = jnp.concatenate(
        [
            embed_weight.transpose(2, 1, 0).reshape(rows, PIX),
            variable_embed.T,
            jnp.zeros((rows, FULL - EXT), bf16),
        ],
        1,
    )
    pad = ((0, 0), (0, FULL - OUTW))
    seed = jnp.pad(cotangent[0].reshape(tokens, OUTW), pad)
    first = lon.first(
        jnp.concatenate([pool_value, pool_out, extended[:, :EXT]], 1),
        jnp.stack([pool_query, first_gain, first_shift, second_gain, second_shift, reduce_bias]),
        rounded(padding[0].reshape(tokens)),
    )
    second = lon.second(jnp.concatenate([attend_out, jnp.pad(head_weight, pad)], 1), seed)
    band = segment[0].reshape(1, tokens).astype(f32)
    columns = lon.columns([(attend_weight, 3), (pool_key, 1), (expand_weight, 1)])
    attend_here, expand_here = columns[:, :FULL], columns[:, FULL:]
    keyed_column = rounded(
        jnp.sum(attend_here[:, 3 * HD :].astype(f32) * lon.own_rows(pool_query).astype(f32), -1)
    )
    keyed_turned = lon.spread_columns(keyed_column)
    keyed_full = keyed_turned.T
    reduce_here = lon.own_rows(reduce_weight)
    expand_bias_here = lon.own_rows(expand_bias)

    plane = field[0]
    border = lax.ppermute(
        rounded(plane[:, 0:1, :]), "lon", [(i, (i - 1) % size) for i in range(size)]
    )
    shifted = jnp.concatenate([rounded(plane[:, 1:, :]), border], axis=1)
    pixels = (
        shifted.reshape(patch_rows, 2, patch_cols, 2, NV)
        .transpose(1, 3, 4, 0, 2)
        .reshape(PIX, tokens)
    )
    pixels = jnp.concatenate(
        [pixels, jnp.ones((NV, tokens), bf16), jnp.zeros((FULL - EXT, tokens), bf16)], 0
    ).astype(f32)

    (
        stream,
        normed_one,
        heads_turned,
        chance,
        value_rows,
        score_weight,
        vectors,
    ) = pool_forward(pixels, keyed_full, position.reshape(tokens, D), first)
    head_full = second[:, HEAD_AT:SEED_AT]
    both = rounded(mm(reduce_here, head_full))
    live = vectors[6:8].reshape(2, H, -1).transpose(1, 0, 2).reshape(H, -1)

    normed_one_all = lon.gather(normed_one, ready=(live, attend_here))
    queries, keys, values = pack(
        order, normed_one_all, attend_here, band, live
    )
    keys_all = lon.gather_far(keys)
    values_all = lon.gather_far(values)
    out, keep, send = attend(queries, keys_all, values_all)
    heads = lon.to_tokens(keep, send)
    stream_one, normed_two = middle(
        order, second, stream, vectors, heads
    )

    key_rows = mm(attend_here[:, 3 * HD :], first[:, 2 * D :], 0, 0)
    normed_two_all = lon.gather(normed_two, ready=(both, expand_here, key_rows))
    grad_before, inner, bias_sums, *parts = feed(
        order,
        normed_two_all,
        expand_here,
        expand_bias_here[None],
        both,
        second,
    )
    terms, sign = lon.sum(parts)
    expand_grad = weight_grad(normed_two_all, [after(grad_before, sign)])
    bias_sums = bias_sums[0]
    grad_one, grad_branch, keep, send, sums, fields = middle_back(
        order,
        second,
        seed,
        after(stream_one, expand_grad),
        vectors,
        terms,
    )
    grad_heads = lon.to_heads(keep, send)
    early_keep, early_send = early_grads(
        order,
        is_first, after(grad_branch, grad_heads[0]), stream_one, vectors, seed, reduce_here, inner, heads
    )
    expand_sum = rounded(region_sum(after(expand_grad, keep), *grad_heads))
    query_back, key_back, value_back = attend_back(
        after(queries, early_keep), out, keys_all, values_all, grad_heads
    )
    key_back, value_back = lon.sum_far(key_back), lon.sum_far(value_back)
    grad_packed, *parts = unpack(
        after(query_back, expand_sum), key_back, value_back, attend_here
    )
    terms, sign = lon.sum(parts)
    early_other = after(region_swap(early_send), sign)
    both_grads = weight_grad(
        normed_one_all, [after(grad_packed, sign)], expand_sum, 3 * HD
    )

    pixel_grad, position_low, *late_parts = pool_backward(
        order,
        pixels,
        score_weight,
        value_rows,
        chance,
        heads_turned,
        keyed_full,
        first,
        stream,
        grad_one,
        vectors,
        after(sums, both_grads),
        early_keep,
        early_other,
        terms,
    )
    moved = lon.rows_back(after(both_grads, *terms))
    late_parts[:4] = after_all(late_parts[:4], *moved)
    position_other = region_swap(position_low)
    late_terms, sign = lon.sum(late_parts, groups=False, ready=(position_other,))
    expand_total, attend_part = lon.shards(after_all(moved, sign))
    attend_total = region_sum(attend_part, *late_terms)
    low = rounded(sum(part.astype(f32) for part in late_terms))
    if lon.own:
        (
            pool_out_total,
            value_total,
            embed_total,
            key_total,
            out_total,
            head_total,
            variable_total,
            *marks,
        ) = finish(is_first, low, region_swap(low), vectors, key_rows)
        marks = [mark.reshape(rows) for mark in marks]
        query_total = marks[5]
    else:
        late_total, early_total = region_both(low, LATE + WIDE)
        pool_out_total, value_total = late_total[:, :D], late_total[:, D : 2 * D]
        embed_total = late_total[:, 2 * D : 2 * D + PIX].T.reshape(4, NV, rows).transpose(1, 0, 2)
        variable_total = late_total[:, 2 * D + PIX : 2 * D + EXT].T
        keyed_total = late_total[:, 2 * D + EXT : LATE]
        key_total = (keyed_total[:, :, None] * vectors[0].reshape(1, H, HD)).reshape(rows, D)
        marks = late_total[:, LATE:].T
        score_total = lon.own_marks(late_total[:, LATE + 8 : LATE + 12])
        query_total = lon.own_shard(jnp.sum(key_rows * score_total.reshape(1, FULL), -1))
        out_total, head_total = early_total[:, :D], early_total[:, D : D + OUTW]

    grad_plane = (
        after(pixel_grad, sign)
        .reshape(2, 2, NV, patch_rows, patch_cols)
        .transpose(3, 0, 4, 1, 2)
        .reshape(2 * patch_rows, 2 * patch_cols, NV)
    )
    returned = lax.ppermute(
        rounded(after(grad_plane[:, -1:, :], sign)), "lon", [(i, (i + 1) % size) for i in range(size)]
    )
    returned = after(returned, *late_terms).astype(f32)
    field_grad = jnp.concatenate([returned, grad_plane[:, :-1, :]], axis=1)[None]

    fields = fields[:, :OUTW].reshape(1, patch_rows, patch_cols, OUTW)

    inner_total = rounded(region_sum(after(inner, sign)))
    reduce_total = lon.own_rows_back(mm(inner_total, head_full, 1, 1))
    bias_total = region_sum(lon.own_rows_back(after(bias_sums, sign)), *late_terms)
    expand_total = expand_total.astype(f32)
    position_total = position_low.astype(f32) + after(position_other, *late_terms).astype(f32)
    position_total = position_total.reshape(patch_rows, patch_cols, D)

    return (
        fields,
        field_grad,
        position_total,
        embed_total,
        variable_total,
        query_total,
        key_total,
        value_total,
        pool_out_total,
        marks[0],
        marks[1],
        attend_total,
        out_total,
        marks[2],
        marks[3],
        expand_total,
        bias_total,
        reduce_total,
        marks[4],
        head_total,
    )


def solution(mesh):
    in_specs = (
        P("dp", None, "lon", None),
        P("dp", None, "lon"),
        P("dp", None, "lon"),
        P(None, "lon", None),
        P(None, None, "lon"),
        P(None, "lon"),
        P("lon"),
        P("lon", None),
        P("lon", None),
        P("lon", None),
        P("lon"),
        P("lon"),
        P("lon", None),
        P("lon", None),
        P("lon"),
        P("lon"),
        P("lon", None),
        P("lon"),
        P("lon", None),
        P("lon"),
        P("lon", None),
        P("dp", None, "lon", None),
    )
    out_specs = (
        P("dp", None, "lon", None),
        P("dp", None, "lon", None),
        P(None, "lon", None),
        P(None, None, "lon"),
        P(None, "lon"),
        P("lon"),
        P("lon", None),
        P("lon", None),
        P("lon", None),
        P("lon"),
        P("lon"),
        P("lon", None),
        P("lon", None),
        P("lon"),
        P("lon"),
        P("lon", None),
        P("lon"),
        P("lon", None),
        P("lon"),
        P("lon", None),
    )
    return jax.shard_map(
        per_device, mesh=mesh, in_specs=in_specs, out_specs=out_specs, check_vma=False
    )
```

```python
import functools

import jax
import jax.numpy as jnp
from jax import lax
from jax.experimental import pallas as pl
from jax.experimental.pallas import tpu as pltpu
from jax.sharding import PartitionSpec as P

D = 1024
H = 16
HD = 64
FF = 4096
NV = 48
OUTW = 192
PIX = 4 * NV
EXT = 5 * NV
FULL = 256
LATE = 2 * D + FULL
HEAD_AT = D
SEED_AT = D + FULL
SHARE = 1
WIDE = 128
SUM_LANE = 67

EPS = 1e-05
NEGATIVE = -1e30
SCALE = HD ** (-0.5)
VMEM = 24 * 1024 * 1024
ROOMY = 56 * 1024 * 1024

f32 = jnp.float32
bf16 = jnp.bfloat16


def rounded(values):
    return values.astype(bf16)


def mm(a, b, da=1, db=0):
    return lax.dot_general(a, b, (((da,), (db,)), ((), ())), preferred_element_type=f32)


def layer_stats(values):
    center = values - jnp.mean(values, -1, keepdims=True)
    spread = lax.rsqrt(jnp.mean(center * center, -1, keepdims=True) + EPS)
    return (center * spread, spread)


def norm_back(grad_normed, normal, spread, gain):
    scaled = grad_normed * gain
    return spread * (
        scaled
        - jnp.mean(scaled, -1, keepdims=True)
        - normal * jnp.mean(scaled * normal, -1, keepdims=True)
    )


def params(limit=VMEM, **more):
    return pltpu.CompilerParams(vmem_limit_bytes=limit, **more)


SMEM_SPEC = pl.BlockSpec(memory_space=pltpu.SMEM)
WHOLE = pl.BlockSpec(memory_space=pltpu.VMEM)


def cost(flops, moved, hard=0, filler=False):
    share = 1 if filler else SHARE
    return pl.CostEstimate(flops=flops // share, bytes_accessed=moved // share, transcendentals=0)


def total(refs):
    return sum(ref[...].astype(f32) for ref in refs)


def pool_forward_kernel(
    pixels_ref,
    keyed_ref,
    position_ref,
    first_ref,
    stream_ref,
    normed_ref,
    heads_ref,
    chance_ref,
    rows_ref,
    score_ref,
    vectors_ref,
):
    pixels = pixels_ref[...]
    blank = jnp.zeros((FULL - EXT, pixels.shape[1]), f32)
    extended = first_ref[:, 2 * D :]
    last = extended[:, FULL - WIDE :].astype(f32)
    vectors_ref[...] = jnp.transpose(last)[WIDE - (FULL - EXT) :, :]
    rows_ref[...] = rounded(mm(first_ref[:, :D], extended, 0, 0))
    score_ref[...] = mm(extended, keyed_ref[...], 0, 0)
    for h in range(H):
        terms = pixels * score_ref[:, h : h + 1]
        scores = terms[:NV]
        for p in range(1, 5):
            scores = scores + terms[p * NV : (p + 1) * NV]
        scores = scores * SCALE
        raised = jnp.exp(scores - jnp.max(scores, 0, keepdims=True))
        chance = raised / jnp.sum(raised, 0, keepdims=True)
        chance_ref[h] = chance
        spread = rounded(jnp.concatenate([chance] * 5 + [blank], 0) * pixels)
        heads_ref[h * HD : (h + 1) * HD, :] = rounded(
            mm(rows_ref[h * HD : (h + 1) * HD, :], spread)
        )
    stream = mm(heads_ref[...], first_ref[:, D : 2 * D], 0, 0) + position_ref[...].astype(f32)
    stream_ref[...] = stream
    normal, unused = layer_stats(stream)
    normed_ref[...] = rounded(normal * vectors_ref[1:2, :] + vectors_ref[2:3, :])


def pool_forward(pixels, keyed, position, first):
    tokens = pixels.shape[1]
    return pl.pallas_call(
        pool_forward_kernel,
        out_shape=(
            jax.ShapeDtypeStruct((tokens, D), f32),
            jax.ShapeDtypeStruct((tokens, D), bf16),
            jax.ShapeDtypeStruct((D, tokens), bf16),
            jax.ShapeDtypeStruct((H, NV, tokens), f32),
            jax.ShapeDtypeStruct((D, FULL), bf16),
            jax.ShapeDtypeStruct((FULL, H), f32),
            jax.ShapeDtypeStruct((FULL - EXT, D), f32),
        ),
        compiler_params=params(ROOMY),
        cost_estimate=cost(3_000_000_000, 8_000_000, H * NV * tokens),
        name="pool_forward",
    )(pixels, keyed, position, first)


def pool_backward_kernel(
    order_ref,
    pixels_ref,
    score_ref,
    rows_ref,
    chance_ref,
    heads_ref,
    keyed_ref,
    first_ref,
    stream_ref,
    grad_one_ref,
    vectors_ref,
    sums_ref,
    early_ref,
    other_ref,
    *refs,
):
    terms, (pixel_ref, stream_grad_ref, *outs), (late, mixed, scores, vectors) = (
        refs[: -6 - H // 2],
        refs[-6 - H // 2 : -4],
        refs[-4:],
    )
    grad_normed = total(terms)
    normal, spread = layer_stats(stream_ref[...])
    grad_stream = grad_one_ref[...] + norm_back(grad_normed, normal, spread, vectors_ref[1:2, :])
    grad_pool = rounded(grad_stream)
    stream_grad_ref[...] = grad_pool
    vectors[...] = jnp.zeros_like(vectors)
    vectors[0:1, :] = jnp.sum(grad_normed * normal, 0, keepdims=True)
    vectors[1:2, :] = jnp.sum(grad_normed, 0, keepdims=True)
    vectors[2:5, :] = sums_ref[0:3, :]
    grad_heads = rounded(mm(first_ref[:, D : 2 * D], grad_pool, 1, 1))
    late[:, :D] = rounded(mm(heads_ref[...], grad_pool))

    pixels = pixels_ref[...]
    tokens = pixels.shape[1]
    blank = jnp.zeros((FULL - EXT, tokens), f32)
    pixel_ref[...] = jnp.zeros_like(pixel_ref)
    scores[...] = jnp.zeros_like(scores)
    late[:, LATE:] = rounded(jnp.transpose(vectors[...]))
    fours = lax.broadcasted_iota(jnp.int32, (HD, FULL), 1) // 4
    fours = rounded(fours == lax.broadcasted_iota(jnp.int32, (HD, FULL), 0))
    lane = lax.broadcasted_iota(jnp.int32, (FULL, WIDE), 1) - 8
    within = lane == lax.broadcasted_iota(jnp.int32, (FULL, WIDE), 0) % 4
    for h in range(H):
        block = slice(h * HD, (h + 1) * HD)
        grad = grad_heads[block, :]
        chance = chance_ref[h]
        wide = jnp.concatenate([chance] * 5 + [blank], 0)
        back = mm(rows_ref[block, :], grad, 0, 0)
        parts = back * pixels
        grad_chance = parts[:NV]
        for p in range(1, 5):
            grad_chance = grad_chance + parts[p * NV : (p + 1) * NV]
        grad_score = chance * (grad_chance - jnp.sum(chance * grad_chance, 0, keepdims=True))
        grad_wide = jnp.concatenate([grad_score * SCALE] * 5 + [blank], 0)
        mixed[block, :] = rounded(mm(grad, rounded(wide * pixels), 1, 1))
        score_grad = jnp.sum(grad_wide * pixels, 1, keepdims=True)
        scores[:, h : h + 1] = score_grad
        late[block, LATE:] += rounded(mm(fours, rounded(jnp.where(within, score_grad, 0.0))))
        pixel_ref[...] += (
            wide[:PIX] * back[:PIX] + grad_wide[:PIX] * score_ref[:PIX, h : h + 1]
        )
    score_grads = rounded(scores[:, :H])
    extended = first_ref[:, 2 * D :]
    late[:, D : 2 * D] = rounded(mm(extended, mixed[...], 1, 1))
    embed_grad = mm(first_ref[:, :D], mixed[...]) + mm(keyed_ref[...], score_grads, 1, 1)
    keyed_grad = mm(extended, score_grads)
    last = jnp.concatenate([keyed_grad, jnp.zeros((D, FULL - H), f32)], 1)
    late[:, 2 * D : LATE] = rounded(
        jnp.where(
            lax.broadcasted_iota(jnp.int32, embed_grad.shape, 1) < EXT,
            embed_grad,
            pltpu.roll(last, EXT, 1),
        )
    )
    for i, ref in enumerate(outs):
        for j in range(2):
            start = pl.multiple_of(order_ref[2 * i + j] * HD, HD)
            ref[j * HD : (j + 1) * HD, : LATE + WIDE] = late[pl.ds(start, HD), :]
        block = slice(2 * i * HD, (2 * i + 2) * HD)
        ref[:, LATE + WIDE :] = rounded(
            early_ref[block, :].astype(f32) + other_ref[block, :].astype(f32)
        )


def pool_backward(
    order, pixels, score, rows, chance, heads, keyed, first, stream, grad_one, vectors, sums, early, other, terms
):
    tokens = pixels.shape[1]
    return pl.pallas_call(
        pool_backward_kernel,
        in_specs=[SMEM_SPEC] + [WHOLE] * (13 + len(terms)),
        out_shape=[
            jax.ShapeDtypeStruct((PIX, tokens), f32),
            jax.ShapeDtypeStruct((tokens, D), bf16),
        ]
        + [jax.ShapeDtypeStruct((2 * HD, LATE + WIDE + early.shape[1]), bf16)] * (H // 2),
        scratch_shapes=[
            pltpu.VMEM((D, LATE + WIDE), bf16),
            pltpu.VMEM((D, FULL), bf16),
            pltpu.VMEM((FULL, WIDE), f32),
            pltpu.VMEM((WIDE, D), f32),
        ],
        compiler_params=params(ROOMY),
        cost_estimate=cost(4_000_000_000, 14_000_000),
        name="pool_backward",
    )(
        order,
        pixels,
        score,
        rows,
        chance,
        heads,
        keyed,
        first,
        stream,
        grad_one,
        vectors,
        sums,
        early,
        other,
        *terms,
    )


def finish_kernel(
    first_ref,
    low_ref,
    other_ref,
    vectors_ref,
    key_ref,
    pool_ref,
    value_ref,
    embed_ref,
    key_grad_ref,
    out_ref,
    head_ref,
    variable_ref,
    *mark_refs,
):
    low, other = low_ref[...].astype(f32), other_ref[...].astype(f32)
    rows = low.shape[0]
    both = low[:, : LATE + WIDE] + other[:, : LATE + WIDE]
    pool_ref[...] = both[:, :D]
    value_ref[...] = both[:, D : 2 * D]
    last = both[:, 2 * D : LATE]
    turned = jnp.transpose(last)
    for p in range(4):
        embed_ref[:, p, :] = turned[p * NV : (p + 1) * NV]
    variable_ref[...] = turned[PIX:EXT]
    lane = lax.broadcasted_iota(jnp.int32, (H, D), 1) // HD
    spread = (lane == lax.broadcasted_iota(jnp.int32, (H, D), 0)).astype(f32)
    key_grad_ref[...] = (
        jnp.dot(
            last[:, EXT:],
            spread,
            precision=lax.Precision.HIGHEST,
            preferred_element_type=f32,
        )
        * vectors_ref[0:1, :]
    )
    marks = both[:, LATE:]
    column = lax.broadcasted_iota(jnp.int32, (rows, FULL), 1)
    scores = jnp.zeros((rows, FULL), f32)
    for c in range(4):
        scores = jnp.where(column % 4 == c, marks[:, 8 + c : 9 + c], scores)
    row = lax.broadcasted_iota(jnp.int32, (rows, FULL), 0)
    scores = jnp.sum(jnp.where(column // 4 == row, scores, 0.0), 0, keepdims=True)
    query = jnp.sum(key_ref[...] * scores, 1, keepdims=True)
    lane = lax.broadcasted_iota(jnp.int32, (rows, WIDE), 1)
    marks = jnp.transpose(jnp.where(lane == 5, query, marks))
    for i, ref in enumerate(mark_refs):
        ref[...] = marks[i : i + 1]
    here, there = low[:, LATE + WIDE :], other[:, LATE + WIDE :]
    is_first = first_ref[0] == 1
    left = jnp.where(is_first, here, there)
    right = jnp.where(is_first, there, here)
    half = left.shape[1]
    out_ref[:, :half] = left
    out_ref[:, half:] = right[:, : D - half]
    head_ref[...] = right[:, D - half : D - half + OUTW]


def finish(is_first, low, other, vectors, key_rows):
    rows = low.shape[0]
    wide = jax.ShapeDtypeStruct((rows, D), f32)
    return pl.pallas_call(
        finish_kernel,
        in_specs=[SMEM_SPEC] + [WHOLE] * 4,
        out_shape=(
            wide,
            wide,
            jax.ShapeDtypeStruct((NV, 4, rows), f32),
            wide,
            wide,
            jax.ShapeDtypeStruct((rows, OUTW), f32),
            jax.ShapeDtypeStruct((NV, rows), f32),
        )
        + (jax.ShapeDtypeStruct((1, rows), f32),) * 6,
        compiler_params=params(),
        cost_estimate=cost(4 * H * D * rows, 3_000_000),
        name="finish",
    )(is_first, low, other, vectors, key_rows)


def shards_kernel(here_ref, there_ref, expand_ref, attend_ref):
    rows, wide = expand_ref.shape[0], FF // H
    for h in range(H):
        block = slice(h * rows, (h + 1) * rows)
        total = here_ref[block, :].astype(f32) + there_ref[block, :].astype(f32)
        expand_ref[:, h * wide : (h + 1) * wide] = total[:, :wide]
        for i in range(3):
            start = i * D + h * HD
            attend_ref[:, start : start + HD] = total[:, wide + i * HD : wide + (i + 1) * HD]


def shards(here, there):
    rows = here.shape[0] // H
    return pl.pallas_call(
        shards_kernel,
        out_shape=(
            jax.ShapeDtypeStruct((rows, FF), f32),
            jax.ShapeDtypeStruct((rows, 3 * D), f32),
        ),
        compiler_params=params(),
        cost_estimate=cost(0, 10_000_000, filler=True),
        name="shards",
    )(here, there)


def copy_parts(refs, into):
    start = 0
    for ref in refs:
        into[start : start + ref.shape[0], :] = ref[...]
        start += ref.shape[0]


def columns_from(rows):
    width = rows[0].shape[1]
    return jnp.concatenate(
        [jnp.transpose(jnp.broadcast_to(row, (width, width))) for row in rows], 0
    )


def pack_kernel(table_ref, weight_ref, band_ref, live_ref, *refs):
    parts, (query_ref, key_ref, value_ref, every) = refs[:-4], refs[-4:]
    copy_parts(parts, every)
    count = every.shape[0]
    block = 512
    blocks = H * block // count
    for i in range(count // block):
        rows = slice(i * block, (i + 1) * block)
        packed = rounded(mm(every[rows, :], weight_ref[...])).astype(f32)
        here = range(i * blocks, (i + 1) * blocks)
        live = columns_from([live_ref[pl.ds(table_ref[e], 1), :] for e in here])
        band = columns_from([band_ref[...]] * blocks)
        left, right = packed[:, :WIDE], packed[:, WIDE:]
        lane = lax.broadcasted_iota(jnp.int32, left.shape, 1)
        query = jnp.where(lane == HD, 1.0 - band, jnp.where(lane == HD + 1, band, 0.0))
        query_ref[rows, :] = rounded(jnp.where(lane < HD, left * SCALE, query))
        key = jnp.where(
            lane == HD,
            NEGATIVE * (1.0 - live * (1.0 - band)),
            jnp.where(
                lane == HD + 1,
                NEGATIVE * (1.0 - live * band),
                jnp.where(lane < HD + 5, -1.0, 0.0),
            ),
        )
        key_ref[rows, :] = rounded(jnp.where(lane < HD, pltpu.roll(left, HD, 1), key))
        value = jnp.where(lane < SUM_LANE, -1.0, jnp.where(lane == SUM_LANE, 1.0, 0.0))
        value_ref[rows, :] = rounded(jnp.where(lane < HD, right, value))


def pack(table, parts, weight, band, live):
    count = sum(part.shape[0] for part in parts)
    return pl.pallas_call(
        pack_kernel,
        in_specs=[SMEM_SPEC] + [WHOLE] * (3 + len(parts)),
        out_shape=[jax.ShapeDtypeStruct((count, WIDE), bf16)] * 3,
        scratch_shapes=[pltpu.VMEM((count, D), bf16)],
        compiler_params=params(),
        cost_estimate=cost(2 * count * D * FULL, 3 * count * D),
        name="pack",
    )(table, weight, band, live, *parts)


def attend_kernel(query_ref, key_ref, value_ref, out_ref, keep_ref, send_ref, *, half):
    scores = mm(query_ref[...], key_ref[...], 1, 1)
    summit = jnp.max(scores, -1, keepdims=True)
    raised = rounded(jnp.exp(scores - summit))
    total = mm(raised, value_ref[...])
    amount = total[:, SUM_LANE : SUM_LANE + 1]
    lane = lax.broadcasted_iota(jnp.int32, total.shape, 1)
    out = jnp.where(lane < HD, total / amount, summit + jnp.log(amount))
    out_ref[...] = out
    low = rounded(out[:, :HD])

    @pl.when(pl.program_id(0) < half)
    def _():
        keep_ref[...] = low

    @pl.when(pl.program_id(0) >= half)
    def _():
        send_ref[...] = low


def attend(queries, keys, values):
    rows, count = queries.shape[0], keys.shape[0]
    block = min(256, max(32, 256 * 2048 // count))
    half = rows // block // 2
    return pl.pallas_call(
        functools.partial(attend_kernel, half=half),
        grid=(2 * half,),
        in_specs=[
            pl.BlockSpec((block, WIDE), lambda i: (i, 0)),
            pl.BlockSpec((count, WIDE), lambda i: (0, 0)),
            pl.BlockSpec((count, WIDE), lambda i: (0, 0)),
        ],
        out_specs=(
            pl.BlockSpec((block, WIDE), lambda i: (i, 0)),
            pl.BlockSpec((block, HD), lambda i: (jnp.minimum(i, half - 1), 0)),
            pl.BlockSpec((block, HD), lambda i: (jnp.maximum(i - half, 0), 0)),
        ),
        out_shape=(
            jax.ShapeDtypeStruct((rows, WIDE), f32),
            jax.ShapeDtypeStruct((rows // 2, HD), bf16),
            jax.ShapeDtypeStruct((rows // 2, HD), bf16),
        ),
        compiler_params=params(dimension_semantics=("arbitrary",)),
        cost_estimate=cost(4 * rows * count * WIDE, rows * WIDE * 6 + count * WIDE * 4),
        name="attend",
    )(queries, keys, values)


def three_parts(values):
    high = rounded(values)
    rest = values - high.astype(f32)
    middle = rounded(rest)
    low = rounded(rest - middle.astype(f32))
    return [part.astype(f32) for part in (high, middle, low)]


def attend_back_kernel(
    query_ref,
    out_ref,
    key_ref,
    value_ref,
    *refs,
):
    moved_refs, (query_grad_ref, key_grad_ref, value_grad_ref, queries, grads) = (
        refs[:-5],
        refs[-5:],
    )

    @pl.when(pl.program_id(0) == 0)
    def _():
        lane = lax.broadcasted_iota(jnp.int32, queries.shape, 1)
        out = out_ref[...]
        log_total = out[:, HD : HD + 1]
        moved = jnp.concatenate([ref[...] for ref in moved_refs], 0).astype(f32)
        grad = jnp.concatenate([moved, pltpu.roll(moved, HD, 1)], 0)
        grad = jnp.where(lane < HD, grad, 0.0)
        balance = jnp.sum(out * grad, -1, keepdims=True)
        query = query_ref[...].astype(f32)
        for i, part in enumerate(three_parts(log_total)):
            query = jnp.where(lane == HD + 2 + i, part, query)
        for i, part in enumerate(three_parts(balance)):
            grad = jnp.where(lane == HD + i, part, grad)
        queries[...] = rounded(query)
        grads[...] = rounded(grad)
        query_grad_ref[...] = jnp.zeros_like(query_grad_ref)

    prob = jnp.exp(mm(key_ref[...], queries[...], 1, 1))
    slope = mm(value_ref[...], grads[...], 1, 1)
    grad_scores = rounded(prob * slope)
    value_grad_ref[...] = mm(rounded(prob), grads[...])
    key_grad_ref[...] = mm(grad_scores, queries[...])
    query_grad_ref[...] += mm(key_ref[...], grad_scores, 0, 0)


def attend_back(queries, out, keys, values, moved):
    rows, count = queries.shape[0], keys.shape[0]
    block = 512
    whole = pl.BlockSpec((rows, WIDE), lambda i: (0, 0))
    part = pl.BlockSpec((block, WIDE), lambda i: (i, 0))
    return pl.pallas_call(
        attend_back_kernel,
        grid=(count // block,),
        in_specs=[
            whole,
            whole,
            part,
            part,
        ]
        + [WHOLE] * len(moved),
        out_specs=(pl.BlockSpec((WIDE, rows), lambda i: (0, 0)), part, part),
        out_shape=(
            jax.ShapeDtypeStruct((WIDE, rows), f32),
            jax.ShapeDtypeStruct((count, WIDE), f32),
            jax.ShapeDtypeStruct((count, WIDE), f32),
        ),
        scratch_shapes=[pltpu.VMEM((rows, WIDE), bf16), pltpu.VMEM((rows, WIDE), bf16)],
        compiler_params=params(dimension_semantics=("arbitrary",)),
        cost_estimate=cost(10 * rows * count * WIDE, rows * WIDE * 12 + count * WIDE * 14),
        name="attend_back",
    )(queries, out, keys, values, *moved)


def unpack_kernel(query_ref, key_ref, value_ref, weight_ref, packed_ref, *refs):
    weight = weight_ref[...]
    step = key_ref.shape[0] // len(refs)
    for i, ref in enumerate(refs):
        rows = slice(i * step, (i + 1) * step)
        query = jnp.transpose(query_ref[:, rows]) * SCALE
        lane = lax.broadcasted_iota(jnp.int32, (step, WIDE), 1)
        left = jnp.where(lane < HD, query, pltpu.roll(key_ref[rows, :], HD, 1))
        right = jnp.where(lane < HD, value_ref[rows, :], 0.0)
        packed = rounded(jnp.concatenate([left, right], 1))
        packed_ref[rows, :] = packed
        ref[...] = rounded(mm(packed, weight, 1, 1))


def unpack(query_back, key_back, value_back, weight):
    count = key_back.shape[0]
    return pl.pallas_call(
        unpack_kernel,
        out_shape=[jax.ShapeDtypeStruct((count, FULL), bf16)]
        + [jax.ShapeDtypeStruct((count // 8, D), bf16)] * 8,
        compiler_params=params(),
        cost_estimate=cost(2 * count * D * FULL, 4 * count * D),
        name="unpack",
    )(query_back, key_back, value_back, weight)


def weight_grad_kernel(beside_ref, *refs, count, width):
    parts, grads, (out_ref, every, changes) = refs[:count], refs[count:-3], refs[-3:]
    left = beside_ref.shape[1] if width else 0
    if left:
        out_ref[:, :left] = beside_ref[...]
    copy_parts(parts, every)
    copy_parts(grads, changes)
    block = 256
    for i in range(D // block):
        columns = slice(i * block, (i + 1) * block)
        grad = rounded(mm(every[:, columns], changes[...], 0, 0))
        out_ref[columns, left:] = grad[:, : out_ref.shape[1] - left]


def weight_grad(parts, grads, beside=None, keep=None):
    count, width = sum(grad.shape[0] for grad in grads), grads[0].shape[1]
    wide = width if beside is None else beside.shape[1] + keep
    return pl.pallas_call(
        functools.partial(
            weight_grad_kernel, count=len(parts), width=0 if beside is None else keep
        ),
        out_shape=jax.ShapeDtypeStruct((D, wide), bf16),
        scratch_shapes=[pltpu.VMEM((count, D), bf16), pltpu.VMEM((count, width), bf16)],
        compiler_params=params(),
        cost_estimate=cost(20 * count * D * width, 3 * count * D, filler=True),
        name="weight_grad",
    )(grads[0] if beside is None else beside, *parts, *grads)


def sort_rows(order_ref, from_ref, into):
    for i in range(H):
        start = pl.multiple_of(order_ref[(i % 2) * 8 + i // 2] * HD, HD)
        into[i * HD : (i + 1) * HD, :] = from_ref[pl.ds(start, HD), :D]


def heads_of(refs):
    return jnp.concatenate([ref[i] for ref in refs for i in range(2)], 1)


def middle_kernel(order_ref, second_ref, stream_ref, vectors_ref, *refs):
    heads, (one_ref, normed_ref, sorted_w) = refs[:-3], refs[-3:]
    sort_rows(order_ref, second_ref, sorted_w)
    stream = stream_ref[...] + mm(heads_of(heads), sorted_w[...])
    one_ref[...] = stream
    normal, unused = layer_stats(stream)
    normed_ref[...] = rounded(normal * vectors_ref[3:4, :] + vectors_ref[4:5, :])


def middle(order, second, stream, vectors, heads):
    tokens = stream.shape[0]
    return pl.pallas_call(
        middle_kernel,
        in_specs=[SMEM_SPEC] + [WHOLE] * (3 + len(heads)),
        out_shape=(
            jax.ShapeDtypeStruct((tokens, D), f32),
            jax.ShapeDtypeStruct((tokens, D), bf16),
        ),
        scratch_shapes=[pltpu.VMEM((D, D), bf16)],
        compiler_params=params(),
        cost_estimate=cost(2 * tokens * D * D, 2 * D * D + 12 * tokens * D),
        name="middle",
    )(order, second, stream, vectors, *heads)


def middle_back_kernel(order_ref, second_ref, seed_ref, stream_ref, vectors_ref, *refs):
    terms, (one_ref, branch_ref, keep_ref, send_ref, sums_ref, fields_ref, sorted_w) = (
        refs[:-7],
        refs[-7:],
    )
    sort_rows(order_ref, second_ref, sorted_w)
    summed = total(terms)
    head = second_ref[:, HEAD_AT:SEED_AT]
    grad_normed = summed[:, :D]
    fields_ref[...] = summed[:, D:] + mm(rounded(stream_ref[...] + vectors_ref[5:6, :]), head)
    stream = stream_ref[...]
    grad_two = rounded(mm(seed_ref[...], head, 1, 1)).astype(f32)
    normal, spread = layer_stats(stream)
    grad_one = grad_two + norm_back(grad_normed, normal, spread, vectors_ref[3:4, :])
    one_ref[...] = grad_one
    branch = rounded(grad_one)
    branch_ref[...] = branch
    back = rounded(mm(branch, sorted_w[...], 1, 1)).astype(f32)
    tokens = stream.shape[0]
    for i in range(H // 2):
        pair = back[:, i * WIDE : (i + 1) * WIDE]
        rows = slice(i * tokens, (i + 1) * tokens)
        keep_ref[rows, :] = rounded(pair[:, :HD])
        send_ref[rows, :] = rounded(pltpu.roll(pair, HD, 1)[:, :HD])
    sums_ref[...] = jnp.zeros_like(sums_ref)
    sums_ref[0:1, :] = jnp.sum(grad_normed * normal, 0, keepdims=True)
    sums_ref[1:2, :] = jnp.sum(grad_normed, 0, keepdims=True)
    sums_ref[2:3, :] = jnp.sum(grad_two, 0, keepdims=True)


def middle_back(order, second, seed, stream, vectors, terms):
    tokens = stream.shape[0]
    half = H // 2 * tokens
    return pl.pallas_call(
        middle_back_kernel,
        in_specs=[SMEM_SPEC] + [WHOLE] * (4 + len(terms)),
        out_shape=(
            jax.ShapeDtypeStruct((tokens, D), f32),
            jax.ShapeDtypeStruct((tokens, D), bf16),
            jax.ShapeDtypeStruct((half, HD), bf16),
            jax.ShapeDtypeStruct((half, HD), bf16),
            jax.ShapeDtypeStruct((8, D), f32),
            jax.ShapeDtypeStruct((tokens, FULL), f32),
        ),
        scratch_shapes=[pltpu.VMEM((D, D), bf16)],
        compiler_params=params(),
        cost_estimate=cost(3 * tokens * D * D, 3 * D * D + 20 * tokens * D),
        name="middle_back",
    )(order, second, seed, stream, vectors, *terms)


def early_kernel(
    order_ref, first_ref, branch_ref, stream_ref, vectors_ref, seed_ref, reduce_ref, inner_ref, *refs
):
    heads, (keep_ref, send_ref, rows) = refs[:-3], refs[-3:]
    branch = branch_ref[...]
    half = keep_ref.shape[1]
    is_first = first_ref[0] == 1
    stream = rounded(stream_ref[...] + vectors_ref[5:6, :])
    rows[...] = mm(stream, seed_ref[...], 0, 0) + mm(reduce_ref[...], inner_ref[...], 0, 0)
    for i in range(H // 2):
        pair = mm(heads[i // 2][i % 2], branch, 0, 0)
        for j in range(2):
            e = j * 8 + i
            start = pl.multiple_of(order_ref[e] * HD, HD)
            here = pair[j * HD : (j + 1) * HD]
            one = here[:, :half]
            two = jnp.concatenate([here[:, half:], rows[pl.ds(start, HD), :]], 1)
            block = slice(e * HD, (e + 1) * HD)
            keep_ref[block, :] = rounded(jnp.where(is_first, one, two))
            send_ref[block, :] = rounded(jnp.where(is_first, two, one))


def early_grads(order, is_first, branch, stream, vectors, seed, reduce_here, inner, heads):
    tokens = stream.shape[0]
    half = (D + FULL) // 2
    return pl.pallas_call(
        early_kernel,
        in_specs=[SMEM_SPEC] * 2 + [WHOLE] * (6 + len(heads)),
        out_shape=(
            jax.ShapeDtypeStruct((D, half), bf16),
            jax.ShapeDtypeStruct((D, half), bf16),
        ),
        scratch_shapes=[pltpu.VMEM((D, FULL), f32)],
        compiler_params=params(ROOMY),
        cost_estimate=cost(20 * tokens * D * (D + FULL), 6_000_000, filler=True),
        name="early_grads",
    )(order, is_first, branch, stream, vectors, seed, reduce_here, inner, *heads)


def feed_kernel(order_ref, expand_ref, bias_ref, both_ref, second_ref, *refs):
    parts, (before_ref, inner_ref, sums_ref, *outs) = refs[:H], refs[H:]
    expand = expand_ref[...]
    both = both_ref[...]
    inner = jnp.zeros(inner_ref.shape, f32)
    sums = jnp.zeros((1, expand.shape[1]), f32)
    tokens = parts[0].shape[0]
    step = 2 * tokens
    for i in range(8):
        block = slice(i * step, (i + 1) * step)
        rows = jnp.concatenate([parts[2 * i][...], parts[2 * i + 1][...]], 0)
        before = mm(rows, expand) + bias_ref[...].astype(f32)
        half = 0.5 + 0.5 * lax.erf(before * 0.7071067811865476)
        hidden = rounded(before * half)
        slope = half + before * jnp.exp(-0.5 * before * before) * 0.3989422804014327
        seed = jnp.concatenate(
            [
                second_ref[pl.ds(pl.multiple_of(order_ref[e] * HD, HD), HD), at : at + FULL]
                for e in (2 * i, 2 * i + 1)
                for at in (SEED_AT, SEED_AT + FULL)
            ],
            0,
        )
        grad = rounded(mm(seed, both, 1, 1) * slope)
        before_ref[block, :] = grad
        outs[i][:, :D] = rounded(mm(grad, expand, 1, 1))
        outs[i][:, D:] = rounded(mm(hidden, both))
        inner = inner + mm(hidden, seed, 0, 0)
        sums = sums + jnp.sum(grad.astype(f32), 0, keepdims=True)
    inner_ref[...] = rounded(inner)
    sums_ref[...] = jnp.broadcast_to(sums, sums_ref.shape)


def feed(order, parts, expand, bias, both, second):
    tokens = parts[0].shape[0]
    count, width = H * tokens, expand.shape[1]
    return pl.pallas_call(
        feed_kernel,
        in_specs=[SMEM_SPEC] + [WHOLE] * (4 + H),
        out_shape=[
            jax.ShapeDtypeStruct((count, width), bf16),
            jax.ShapeDtypeStruct((width, FULL), bf16),
            jax.ShapeDtypeStruct((8, width), f32),
        ]
        + [jax.ShapeDtypeStruct((2 * tokens, D + FULL), bf16)] * 8,
        compiler_params=params(),
        cost_estimate=cost(6 * count * D * width, 5 * count * D),
        name="feed",
    )(order, expand, bias, both, second, *parts)


def turn(array, pairs):
    return lax.ppermute(array, "lon", pairs)


class Steps:
    def __init__(self, lon, ready):
        self.lon, self.ready = lon, ready
        self.side, self.mine, self.low, self.sent = {}, {}, {}, {}

    def add(self, k, keep, send):
        rows = keep.shape[0] // 2
        came = turn(send, self.lon.core)
        away = rounded(keep[rows:].astype(f32) + came[rows:].astype(f32))
        if k in (3, 0):
            away = after(away, self.low[2], *self.ready.get(k, ()))
        self.side[k] = turn(away, self.lon.side)
        self.mine[k] = (
            keep[:rows].astype(f32) + came[:rows].astype(f32) + self.side[k].astype(f32)
        )
        if k:
            self.low[k] = rounded(self.mine[k])
            self.sent[k] = turn(self.low[k], self.lon.up[k])

    def terms(self):
        return [self.mine[0], self.sent[1], self.sent[2], self.sent[3]]


class Lon:
    def __init__(self, size):
        self.size = size
        self.groups = size // H
        self.near = [[g * H + h for h in range(H)] for g in range(self.groups)]
        self.far = [[g * H + h for g in range(self.groups)] for h in range(H)]
        self.own = self.groups == 1
        every = range(H)
        self.core = [(i, i ^ 1) for i in every]
        self.side = [(i, i ^ 2) for i in every]
        self.down = [[(i, (i + 4 * k) % H) for i in every] for k in range(4)]
        self.up = [[(i, (i - 4 * k) % H) for i in every] for k in range(4)]

    def split(self):
        return {"axis_index_groups": self.near}

    def order(self):
        if not self.own:
            return jnp.arange(H, dtype=jnp.int32)
        here = lax.axis_index("lon")
        z, x, core = here // 4, (here // 2) % 2, here % 2
        return jnp.stack(
            [
                ((z - k) % 4) * 4 + (x ^ xr) * 2 + (core ^ cr)
                for cr in range(2)
                for k in range(4)
                for xr in range(2)
            ]
        ).astype(jnp.int32)

    def gather_all(self, part):
        return lax.all_gather(part, "lon", axis=0, tiled=True)

    def sum_all(self, whole):
        return lax.psum_scatter(whole, "lon", scatter_dimension=0, tiled=True)

    def gather(self, part, groups=True, ready=()):
        if not self.own:
            split = self.split() if groups else {}
            whole = lax.all_gather(part, "lon", axis=0, tiled=True, **split)
            rows = whole.shape[0] // H
            return [whole[i * rows : (i + 1) * rows] for i in range(H)]
        line = {0: part, 1: turn(part, self.down[1]), 3: turn(part, self.down[3])}
        side = {0: turn(part, self.side)}
        line[2] = turn(after(part, line[1], line[3], *ready), self.down[2])
        for k in (1, 3, 2):
            side[k] = turn(line[k], self.side)
        mine = [piece for k in range(4) for piece in (line[k], side[k])]
        return mine + [turn(piece, self.core) for piece in mine]

    def gather_group(self, part):
        return lax.all_gather(part, "lon", axis=0, tiled=True, **({} if self.own else self.split()))

    def sum(self, parts, groups=True, ready={}):
        if not self.own:
            whole = jnp.concatenate(parts)
            split = self.split() if groups else {}
            whole = lax.psum_scatter(whole, "lon", scatter_dimension=0, tiled=True, **split)
            return [whole], whole
        steps = Steps(self, ready)
        for k in (2, 1, 3, 0):
            steps.add(k, parts[k], parts[4 + k])
        return steps.terms(), steps.side[0]

    def first(self, weights, vectors, live):
        spare = FULL - EXT
        if not self.own:
            vectors = lax.all_gather(vectors, "lon", axis=1, tiled=True)
            live = self.gather_group(live).reshape(H, 2, HD).transpose(1, 0, 2)
        marks = jnp.concatenate([vectors, live.reshape(2, -1)]).T
        marks = jnp.pad(marks, ((0, 0), (0, spare - marks.shape[1])))
        if not self.own:
            return jnp.concatenate([self.gather_all(weights), marks], 1)
        return self.gather_all(jnp.concatenate([weights, marks], 1))

    def second(self, weights, seed):
        if not self.own:
            seed = self.gather_group(seed).reshape(H, 2, HD, FULL).transpose(0, 2, 1, 3)
            return jnp.concatenate([self.gather_all(weights), seed.reshape(D, 2 * FULL)], 1)
        half = seed.shape[0] // 2
        return self.gather_all(jnp.concatenate([weights, seed[:half], seed[half:]], 1))

    def spread_columns(self, column):
        if self.own:
            return self.swap_all(jnp.tile(column[None], (H, 1)))
        return lax.all_gather(column, "lon", axis=0, **self.split())

    def own_marks(self, rows):
        if self.own:
            return rows
        every = self.gather_all(rows)
        return lax.dynamic_slice_in_dim(every, self.head() * HD, HD, 0)

    def own_shard(self, block):
        if self.own:
            return block
        every = lax.all_gather(block, "lon", axis=0, tiled=True, **self.split())
        count = D // self.size
        return lax.dynamic_slice_in_dim(every, lax.axis_index("lon") * count, count, 0)

    def swap_all(self, whole):
        return lax.all_to_all(whole, "lon", 0, 0, tiled=True)

    def swap(self, keep, send):
        rows = keep.shape[0] // 8
        both = jnp.concatenate([keep, turn(send, self.core)], 1).reshape(4, 2, rows, WIDE)
        came = turn(both[:, 1], self.side)
        ready = [jnp.stack([both[k, 0], came[k]]) for k in range(4)]
        return ready[:1] + [turn(ready[4 - k], self.up[4 - k]) for k in range(1, 4)]

    def to_tokens(self, keep, send):
        if self.own:
            return self.swap(keep, send)
        part = jnp.concatenate([keep, send])
        moved = lax.all_to_all(part, "lon", 0, 0, tiled=True, **self.split())
        moved = moved.reshape(H, -1, HD)
        moved = jnp.concatenate([moved[: H // 2], moved[H // 2 :]], -1)
        return [moved[2 * k : 2 * k + 2] for k in range(4)]

    def to_heads(self, keep, send):
        rows = keep.shape[0] // 4
        if self.own:
            return [part.reshape(rows, WIDE) for part in self.swap(keep, send)]
        moved = jnp.concatenate([keep, send])
        moved = lax.all_to_all(moved, "lon", 0, 0, tiled=True, **self.split())
        moved = jnp.concatenate([moved[: keep.shape[0]], moved[keep.shape[0] :]], 1)
        return [moved[k * rows : (k + 1) * rows] for k in range(4)]

    def gather_far(self, part):
        if self.own:
            return part
        return lax.all_gather(part, "lon", axis=0, tiled=True, axis_index_groups=self.far)

    def sum_far(self, whole):
        if self.own:
            return whole
        return lax.psum_scatter(
            whole, "lon", scatter_dimension=0, tiled=True, axis_index_groups=self.far
        )

    def head(self):
        return lax.rem(lax.axis_index("lon"), H)

    def columns(self, parts):
        if not self.own:
            parts = [(self.gather_all(part), blocks) for part, blocks in parts]
        rows = parts[0][0].shape[0]
        cut = [part.reshape(rows, blocks, H, -1) for part, blocks in parts]
        if self.own:
            cut = [part.transpose(2, 0, 1, 3).reshape(H * rows, -1) for part in cut]
            return self.swap_all(jnp.concatenate(cut, 1))
        mine = [lax.dynamic_index_in_dim(part, self.head(), 2, keepdims=False) for part in cut]
        return jnp.concatenate([part.reshape(rows, -1) for part in mine], 1)

    def rows_back(self, block):
        if self.own:
            return [self.swap_all(block)]
        rows, wide = block.shape[0], FF // H
        totals = []
        for part, blocks in ((block[:, :wide], 1), (block[:, wide:], 3)):
            whole = jnp.zeros((rows, blocks, H, part.shape[1] // blocks), f32)
            whole = lax.dynamic_update_index_in_dim(
                whole, part.astype(f32).reshape(rows, blocks, -1), self.head(), 2
            )
            totals.append(rounded(self.sum_all(whole.reshape(rows, -1))))
        return totals

    def shards(self, here, there):
        if self.own:
            return shards(here[0], there[0])
        return [a.astype(f32) + b.astype(f32) for a, b in zip(here, there)]

    def own_rows(self, part):
        if self.own:
            return part
        every = self.gather_all(part)
        rows = every.shape[0] // H
        return lax.dynamic_slice_in_dim(every, self.head() * rows, rows, 0)

    def own_rows_back(self, block):
        if self.own:
            return block
        whole = jnp.zeros((block.shape[0] * H,) + block.shape[1:], f32)
        whole = lax.dynamic_update_slice_in_dim(whole, block, self.head() * block.shape[0], 0)
        return self.sum_all(whole)


def after(value, *earlier):
    return lax.optimization_barrier((value,) + earlier)[0]


def region_swap(part):
    return lax.ppermute(part, "dp", [(0, 1), (1, 0)])


def region_both(part, width):
    other = region_swap(part)
    is_first = lax.axis_index("dp") == 0
    here, there = part[:, width:], other[:, width:]
    sides = [jnp.where(is_first, here, there), jnp.where(is_first, there, here)]
    return (
        part[:, :width].astype(f32) + other[:, :width].astype(f32),
        jnp.concatenate(sides, 1).astype(f32),
    )


def after_all(values, *earlier):
    return lax.optimization_barrier(tuple(values) + earlier)[: len(values)]


def quarter(blocks, k):
    return [blocks[8 * cr + 2 * k + xr] for cr in range(2) for xr in range(2)]


def region_sum(part, *earlier):
    low = rounded(part)
    if lax.axis_size("dp") == 2:
        other = after(region_swap(low), *earlier)
        return low.astype(f32) + other.astype(f32)
    return lax.psum(low, "dp").astype(f32)


def per_device(
    field,
    segment,
    padding,
    position,
    embed_weight,
    variable_embed,
    pool_query,
    pool_key,
    pool_value,
    pool_out,
    first_gain,
    first_shift,
    attend_weight,
    attend_out,
    second_gain,
    second_shift,
    expand_weight,
    expand_bias,
    reduce_weight,
    reduce_bias,
    head_weight,
    cotangent,
):
    size = lax.axis_size("lon")
    lon = Lon(size)
    rows = pool_value.shape[0]
    patch_rows, patch_cols = position.shape[0], position.shape[1]
    tokens = patch_rows * patch_cols
    many = H * tokens
    order = lon.order()
    is_first = (lax.axis_index("dp") == 0).astype(jnp.int32).reshape(1)

    extended = jnp.concatenate(
        [
            embed_weight.transpose(2, 1, 0).reshape(rows, PIX),
            variable_embed.T,
            jnp.zeros((rows, FULL - EXT), bf16),
        ],
        1,
    )
    pad = ((0, 0), (0, FULL - OUTW))
    seed = jnp.pad(cotangent[0].reshape(tokens, OUTW), pad)
    first = lon.first(
        jnp.concatenate([pool_value, pool_out, extended[:, :EXT]], 1),
        jnp.stack([pool_query, first_gain, first_shift, second_gain, second_shift, reduce_bias]),
        rounded(padding[0].reshape(tokens)),
    )
    second = lon.second(jnp.concatenate([attend_out, jnp.pad(head_weight, pad)], 1), seed)
    band = segment[0].reshape(1, tokens).astype(f32)
    columns = lon.columns([(attend_weight, 3), (pool_key, 1), (expand_weight, 1)])
    attend_here, expand_here = columns[:, :FULL], columns[:, FULL:]
    keyed_column = rounded(
        jnp.sum(attend_here[:, 3 * HD :].astype(f32) * lon.own_rows(pool_query).astype(f32), -1)
    )
    keyed_turned = lon.spread_columns(keyed_column)
    keyed_full = keyed_turned.T
    reduce_here = lon.own_rows(reduce_weight)
    expand_bias_here = lon.own_rows(expand_bias)

    plane = field[0]
    border = lax.ppermute(
        rounded(plane[:, 0:1, :]), "lon", [(i, (i - 1) % size) for i in range(size)]
    )
    shifted = jnp.concatenate([rounded(plane[:, 1:, :]), border], axis=1)
    pixels = (
        shifted.reshape(patch_rows, 2, patch_cols, 2, NV)
        .transpose(1, 3, 4, 0, 2)
        .reshape(PIX, tokens)
    )
    pixels = jnp.concatenate(
        [pixels, jnp.ones((NV, tokens), bf16), jnp.zeros((FULL - EXT, tokens), bf16)], 0
    ).astype(f32)

    (
        stream,
        normed_one,
        heads_turned,
        chance,
        value_rows,
        score_weight,
        vectors,
    ) = pool_forward(pixels, keyed_full, position.reshape(tokens, D), first)
    head_full = second[:, HEAD_AT:SEED_AT]
    both = rounded(mm(reduce_here, head_full))
    live = vectors[6:8].reshape(2, H, -1).transpose(1, 0, 2).reshape(H, -1)

    normed_one_all = lon.gather(normed_one, ready=(live, attend_here))
    queries, keys, values = pack(
        order, normed_one_all, attend_here, band, live
    )
    keys_all = lon.gather_far(keys)
    values_all = lon.gather_far(values)
    out, keep, send = attend(queries, keys_all, values_all)
    heads = lon.to_tokens(keep, send)
    stream_one, normed_two = middle(
        order, second, stream, vectors, heads
    )

    key_rows = mm(attend_here[:, 3 * HD :], first[:, 2 * D :], 0, 0)
    normed_two_all = lon.gather(normed_two, ready=(both, expand_here, key_rows))
    grad_before, inner, bias_sums, *parts = feed(
        order,
        normed_two_all,
        expand_here,
        expand_bias_here[None],
        both,
        second,
    )
    terms, sign = lon.sum(parts)
    expand_grad = weight_grad(normed_two_all, [after(grad_before, sign)])
    bias_sums = bias_sums[0]
    grad_one, grad_branch, keep, send, sums, fields = middle_back(
        order,
        second,
        seed,
        after(stream_one, expand_grad),
        vectors,
        terms,
    )
    grad_heads = lon.to_heads(keep, send)
    early_keep, early_send = early_grads(
        order,
        is_first, after(grad_branch, grad_heads[0]), stream_one, vectors, seed, reduce_here, inner, heads
    )
    query_back, key_back, value_back = attend_back(
        after(queries, early_keep), out, keys_all, values_all, grad_heads
    )
    key_back, value_back = lon.sum_far(key_back), lon.sum_far(value_back)
    grad_packed, *parts = unpack(
        query_back, key_back, value_back, attend_here
    )
    terms, sign = lon.sum(parts)
    early_other = after(region_swap(early_send), sign)
    both_grads = weight_grad(
        normed_one_all, [after(grad_packed, sign)], expand_grad, 3 * HD
    )

    pixel_grad, position_low, *late_parts = pool_backward(
        order,
        pixels,
        score_weight,
        value_rows,
        chance,
        heads_turned,
        keyed_full,
        first,
        stream,
        grad_one,
        vectors,
        after(sums, both_grads),
        early_keep,
        early_other,
        terms,
    )
    grad_plane = (
        pixel_grad.reshape(2, 2, NV, patch_rows, patch_cols)
        .transpose(3, 0, 4, 1, 2)
        .reshape(2 * patch_rows, 2 * patch_cols, NV)
    )
    returned = lax.ppermute(
        rounded(grad_plane[:, -1:, :]), "lon", [(i, (i + 1) % size) for i in range(size)]
    )
    moved = lon.rows_back(after(both_grads, *terms))
    late_parts[:4] = after_all(late_parts[:4], *moved)
    moved_other = [region_swap(part) for part in moved]
    position_other = region_swap(position_low)
    late_terms, sign = lon.sum(
        late_parts, groups=False, ready={3: [position_other], 0: moved_other + [returned]}
    )
    expand_total, attend_total = lon.shards(after_all(moved, *late_terms[:2]), moved_other)
    low = rounded(sum(part.astype(f32) for part in late_terms))
    if lon.own:
        (
            pool_out_total,
            value_total,
            embed_total,
            key_total,
            out_total,
            head_total,
            variable_total,
            *marks,
        ) = finish(is_first, low, region_swap(low), vectors, key_rows)
        marks = [mark.reshape(rows) for mark in marks]
        query_total = marks[5]
    else:
        late_total, early_total = region_both(low, LATE + WIDE)
        pool_out_total, value_total = late_total[:, :D], late_total[:, D : 2 * D]
        embed_total = late_total[:, 2 * D : 2 * D + PIX].T.reshape(4, NV, rows).transpose(1, 0, 2)
        variable_total = late_total[:, 2 * D + PIX : 2 * D + EXT].T
        keyed_total = late_total[:, 2 * D + EXT : LATE]
        key_total = (keyed_total[:, :, None] * vectors[0].reshape(1, H, HD)).reshape(rows, D)
        marks = late_total[:, LATE:].T
        score_total = lon.own_marks(late_total[:, LATE + 8 : LATE + 12])
        query_total = lon.own_shard(jnp.sum(key_rows * score_total.reshape(1, FULL), -1))
        out_total, head_total = early_total[:, :D], early_total[:, D : D + OUTW]

    returned = after(returned, *late_terms).astype(f32)
    field_grad = jnp.concatenate([returned, grad_plane[:, :-1, :]], axis=1)[None]

    fields = fields[:, :OUTW].reshape(1, patch_rows, patch_cols, OUTW)

    inner_total = rounded(region_sum(after(inner, sign)))
    reduce_total = lon.own_rows_back(mm(inner_total, head_full, 1, 1))
    bias_total = region_sum(lon.own_rows_back(after(bias_sums, sign)), *late_terms)
    position_total = position_low.astype(f32) + after(position_other, *late_terms).astype(f32)
    position_total = position_total.reshape(patch_rows, patch_cols, D)

    return (
        fields,
        field_grad,
        position_total,
        embed_total,
        variable_total,
        query_total,
        key_total,
        value_total,
        pool_out_total,
        marks[0],
        marks[1],
        attend_total,
        out_total,
        marks[2],
        marks[3],
        expand_total,
        bias_total,
        reduce_total,
        marks[4],
        head_total,
    )


def solution(mesh):
    in_specs = (
        P("dp", None, "lon", None),
        P("dp", None, "lon"),
        P("dp", None, "lon"),
        P(None, "lon", None),
        P(None, None, "lon"),
        P(None, "lon"),
        P("lon"),
        P("lon", None),
        P("lon", None),
        P("lon", None),
        P("lon"),
        P("lon"),
        P("lon", None),
        P("lon", None),
        P("lon"),
        P("lon"),
        P("lon", None),
        P("lon"),
        P("lon", None),
        P("lon"),
        P("lon", None),
        P("dp", None, "lon", None),
    )
    out_specs = (
        P("dp", None, "lon", None),
        P("dp", None, "lon", None),
        P(None, "lon", None),
        P(None, None, "lon"),
        P(None, "lon"),
        P("lon"),
        P("lon", None),
        P("lon", None),
        P("lon", None),
        P("lon"),
        P("lon"),
        P("lon", None),
        P("lon", None),
        P("lon"),
        P("lon"),
        P("lon", None),
        P("lon"),
        P("lon", None),
        P("lon"),
        P("lon", None),
    )
    return jax.shard_map(
        per_device, mesh=mesh, in_specs=in_specs, out_specs=out_specs, check_vma=False
    )
```
